32 devices in a mesh: loc: 8 (over z, core), inc: 4 (over y, x).
Axes of the slice: x: 2, y: 2, z: 4, core: 2. Of those that a mesh axis runs over, the one named last changes fastest.
Arguments:
- cont_value: float32 [3200, 8192], P('loc', 'inc'), may hold values from -4 to 252, as said below
- flow_util: float32 [3200, 8192], P('loc', 'inc'), may hold values from -6 to 6
- move_cost: float32 [3200, 3200], P('loc'), may hold values from 0 to 6, as said below
- live_mask: int32 [3200], P('loc'), may hold values 0 or 1
- trans_weight: float32 [128, 128], replicated, may hold values from 0.02 to 1
- asset_policy: int32 [128, 64], replicated, may hold values from 0 to 63
- mass: float32 [3200, 8192], P('loc', 'inc'), may hold values from 0.1 to 1
Outputs:
- new_value: float32 [3200, 8192], P('loc', 'inc')
- new_mass: float32 [3200, 8192], P('loc', 'inc')
The draws below stay inside these ranges and needn't reach their ends.
Inputs may be any that keep to these rules, and one draw needn't show every extreme that they name: cont_value lies within the stated bounds. move_cost is symmetric with a zero diagonal; off the diagonal it lies between 0.5 and 6.
All inputs are finite; a program needn't handle non-finite values. No bound on the sum of `live_mask` on one device may be relied on, other than what follows from the above.
Results may differ from the reference program's by a relative error of at most 0.004.
Values may be sent and summed in bfloat16 or wider, within the bound.
No kernel may reach another device: no remote copies, remote signals or barrier semaphores. Data moves between devices by JAX's collectives and lax.ppermute only.
A program may use at most 64 MiB of HBM per device.

```python
import math
import jax
import jax.numpy as jnp
from jax import lax

L = 3200
E = 128
A = 64
S = 8192


def draw_cont_value(key, part):
    key_base = jax.random.fold_in(key, 0)
    key_effect = jax.random.fold_in(key, 4)
    effect = 1.2 * jax.random.normal(key_effect, (L, 1), jnp.float32)
    noise = 0.8 * jax.random.normal(key_base, (L, E * A), jnp.float32)
    return jnp.clip(effect + noise, -4.0, 4.0)


def draw_move_cost(key, part):
    key_center, key_member, key_place = jax.random.split(key, 3)
    clusters = max(4, L // 64)
    slope, spread = (10.0, 0.05)
    centers = jax.random.uniform(key_center, (clusters, 2), jnp.float32, 0.0, 1.0)
    member = jax.random.randint(key_member, (L,), 0, clusters)
    coords = centers[member] + spread * jax.random.normal(key_place, (L, 2), jnp.float32)
    along_x = coords[:, 0][:, None] - coords[:, 0][None, :]
    along_y = coords[:, 1][:, None] - coords[:, 1][None, :]
    distance = jnp.sqrt(along_x * along_x + along_y * along_y)
    cost = jnp.clip(0.5 + slope * distance, 0.5, 6.0)
    return cost * (1.0 - jnp.eye(L, dtype=jnp.float32))


def touch_ends(values, own_key, least, largest):
    index_at = [jax.random.randint(jax.random.fold_in(own_key, axis), (), 0, length) for axis, length in enumerate(values.shape)]
    longest = values.shape.index(max(values.shape))
    next_to = index_at[:longest] + [(index_at[longest] + 1) % values.shape[longest]] + index_at[longest + 1:]
    return values.at[tuple(index_at)].set(least).at[tuple(next_to)].set(largest)


def level_of(key, dims, shards, smallest, top_value):
    loudness, own = 1.0, jax.random.fold_in(key, 6)
    for position, shards_of in shards:
        steps = jnp.exp(jax.random.uniform(jax.random.fold_in(own, position), (shards_of,), jnp.float32, smallest / len(shards), top_value / len(shards)))
        loudness = loudness * jnp.repeat(steps, dims[position] // shards_of).reshape([-1 if axis == position else 1 for axis in range(len(dims))])
    return loudness


def normal_values(own_key, shape, deviation, bound, cuts=(), held_as=jnp.bfloat16):
    loudness = level_of(own_key, shape, cuts, -0.22, 0.18) if cuts else 1.0
    result = jax.random.normal(own_key, shape, jnp.float32) * deviation * loudness
    return jnp.minimum(jnp.maximum(result, -bound), bound).astype(held_as)


def setup_inputs(seed: int = 0) -> dict:
    streams_of = jax.random.split(jax.random.key(seed), 8)
    return {
        "cont_value": draw_cont_value(jax.random.fold_in(streams_of[7], 71), 0),
        "flow_util": normal_values(streams_of[1], (L, S), 1.0, 6.0, ((0, 8), (1, 4)), jnp.float32),
        "move_cost": draw_move_cost(jax.random.fold_in(streams_of[7], 71), 0),
        "live_mask": touch_ends((jax.random.randint(streams_of[3], (L,), 0, 16) < 15).astype(jnp.int32), jax.random.fold_in(streams_of[3], 1), 0, 1),
        "trans_weight": jnp.clip(jnp.exp(jax.random.uniform(streams_of[4], (E, E), jnp.float32, math.log(0.02), math.log(1.0))), 0.02, 1.0),
        "asset_policy": touch_ends(jax.random.randint(streams_of[5], (E, A), 0, A), jax.random.fold_in(streams_of[5], 1), 0, A - 1).astype(jnp.int32),
        "mass": jnp.clip(jnp.exp(math.log(1.0) - 2.3025851 * jax.random.uniform(streams_of[6], (L, S), jnp.float32) ** level_of(streams_of[6], (L, S), ((0, 8), (1, 4)), -0.2, 0.2)), 0.1, 1.0),
    }


DISCOUNT = 0.96


def reference(cont_value, flow_util, move_cost, live_mask, trans_weight, asset_policy, mass):
    high = lax.Precision.HIGHEST
    eye_full = jnp.eye(E, dtype=jnp.float32)
    raised = trans_weight + 16.0 * eye_full
    trans_prob = raised / jnp.sum(raised, axis=1, keepdims=True)
    onehot = (asset_policy[:, :, None] == jnp.arange(A, dtype=jnp.int32)[None, None, :]).astype(jnp.float32)
    value_grid = cont_value.reshape(L, E, A)
    expect = jnp.einsum('ef,jfb->jeb', trans_prob, value_grid, precision=high)
    chosen = jnp.einsum('jeb,eab->jea', expect, onehot, precision=high).reshape(L, E * A)
    scores = DISCOUNT * chosen
    live_rows = live_mask[:, None] > 0
    column_max = jnp.max(jnp.where(live_rows, scores, jnp.float32(-1e30)), axis=0)
    dest_weight = jnp.where(live_rows, jnp.exp(scores - column_max[None, :]), jnp.float32(0.0)).astype(jnp.bfloat16)
    kernel = jnp.exp(-move_cost).astype(jnp.bfloat16)
    kernel_wide = kernel.astype(jnp.float32)
    totals = jnp.dot(kernel_wide, dest_weight.astype(jnp.float32), precision=high)
    new_value = flow_util + column_max[None, :] + jnp.log(totals)
    shares = (mass / totals).astype(jnp.bfloat16)
    arrived = jnp.dot(kernel_wide.T, shares.astype(jnp.float32), precision=high)
    movers = dest_weight.astype(jnp.float32) * arrived
    shuffled = jnp.einsum('jea,eab->jeb', movers.reshape(L, E, A), onehot, precision=high)
    new_mass = jnp.einsum('ef,jeb->jfb', trans_prob, shuffled, precision=high).reshape(L, E * A)
    return new_value, new_mass
```

```python
import functools
import math

import jax
import jax.numpy as jnp
from jax import lax
from jax.experimental import pallas as pl
from jax.experimental.pallas import tpu as pltpu
from jax.sharding import PartitionSpec as P

DISCOUNT = 0.96
LANES = 128
TILE = 16
VALUE_LOW = -4.0
VALUE_HIGH = 252.0
STEP = (VALUE_HIGH - VALUE_LOW) / 65535.0
HALF = 32768.0
LN2 = math.log(2.0)
SCORE_STEP = DISCOUNT * STEP / LN2
SCORE_SHIFT = DISCOUNT * (HALF * STEP + VALUE_LOW)

BF = jnp.bfloat16
F32 = jnp.float32
VMEM = pl.BlockSpec(memory_space=pltpu.VMEM)
SMEM = pl.BlockSpec(memory_space=pltpu.SMEM)
ANY = pl.BlockSpec(memory_space=pl.ANY)


def dot(a, b):
    return lax.dot_general(a, b, (((1,), (0,)), ((), ())), preferred_element_type=F32)


def dot_nt(a, b):
    return lax.dot_general(a, b, (((1,), (1,)), ((), ())), preferred_element_type=F32)


def lanes_at(start, size):
    return pl.ds(pl.multiple_of(start, LANES), size)


def call(kernel, outs, ins, scratch=(), flops=0, specs=None, vmem=48):
    moved = sum(math.prod(x.shape) * x.dtype.itemsize for x in list(ins) + list(outs))
    return pl.pallas_call(
        kernel,
        out_shape=tuple(outs),
        in_specs=specs or [SMEM] + [VMEM] * (len(ins) - 1),
        out_specs=tuple([VMEM] * len(outs)),
        scratch_shapes=list(scratch),
        compiler_params=pltpu.CompilerParams(vmem_limit_bytes=vmem * 1024 * 1024),
        cost_estimate=pl.CostEstimate(flops=flops, bytes_accessed=moved, transcendentals=0),
    )(*ins)


class Plan:
    def __init__(self, n_loc, n_inc, counties, rows, columns, incomes, assets):
        self.n_loc, self.n_inc = n_loc, n_inc
        self.counties, self.rows, self.columns = counties, rows, columns
        self.incomes, self.assets = incomes, assets
        self.own_incomes = incomes // n_inc
        self.own_assets = assets // n_inc
        self.group_assets = LANES // self.own_incomes
        self.groups = self.own_assets // max(self.group_assets, 1)
        self.wide = n_inc * LANES
        self.part = columns // n_inc
        self.states = columns // n_loc
        self.packed = rows + TILE
        self.block_rows = counties // LANES
        self.window = (self.block_rows // 2 + 1) * LANES
        self.stride = rows // n_inc // TILE * TILE
        self.quarter = rows - self.stride * (n_inc - 1)

    def fits(self):
        power = lambda n: n & (n - 1) == 0
        return (
            power(self.n_loc)
            and power(self.n_inc)
            and self.incomes == LANES
            and self.own_incomes * self.group_assets == LANES
            and self.groups * self.group_assets == self.own_assets
            and self.groups == self.n_inc
            and self.states % LANES == 0
            and self.rows % TILE == 0
            and self.counties % LANES == 0
            and self.block_rows % 2 == 1
        )


def order_maps(plan):
    w, oa, oi = plan.wide, plan.own_assets, plan.own_incomes
    r = lax.broadcasted_iota(jnp.int32, (w, w), 0)
    c = lax.broadcasted_iota(jnp.int32, (w, w), 1)
    a = plan.assets
    spot = (r % a) // oa * LANES + r // a * oa + r % oa
    first = (c == spot).astype(BF)
    second = (c == r % oa * oi + r // oa).astype(BF)
    return first, second


def encode_kernel(plan, at, value, first, second, *refs):
    outs, (high, low) = refs[: plan.n_inc], refs[plan.n_inc :]
    inc, w = at[1], plan.wide
    for t in range(plan.n_inc):
        x = value[:, t * w : (t + 1) * w]
        code = jnp.clip(jnp.round((x - VALUE_LOW) * (1.0 / STEP)) - HALF, -HALF, HALF - 1.0)
        top = jnp.floor(code * (1.0 / 256.0))
        rest = code - 256.0 * top
        moved_top = dot(top.astype(BF), first[...]).astype(BF)
        moved_rest = dot(rest.astype(BF), first[...]).astype(BF)
        for q in range(plan.n_inc):
            high[q, :, t * LANES : (t + 1) * LANES] = moved_top[:, q * LANES : (q + 1) * LANES]
            low[q, :, t * LANES : (t + 1) * LANES] = moved_rest[:, q * LANES : (q + 1) * LANES]
    for k in range(plan.n_inc):
        q = inc ^ k
        code = dot(high[q], second[...]) * 256.0 + dot(low[q], second[...])
        outs[k][...] = code.astype(jnp.int32).astype(jnp.int16)


def weight_kernel(plan, at, *refs):
    ni, nl, rows = plan.n_inc, plan.n_loc, plan.rows
    codes, (mix_a, mix_b, live), refs = refs[:ni], refs[ni : ni + 3], refs[ni + 3 :]
    outs, (held, weights) = refs[:nl], refs[nl:]
    loc, inc, w = at[0], at[1], plan.wide
    alive = live[...] > 0.0
    for g in range(plan.groups):
        for k in range(ni):
            held[:, lanes_at((inc ^ k) * LANES, LANES)] = codes[k][
                :, g * LANES : (g + 1) * LANES
            ].astype(jnp.int32)
        code = held[...]
        top = (code >> 8).astype(F32).astype(BF)
        rest = (code & 255).astype(F32).astype(BF)
        mixed = (dot(top, mix_a[...]) + dot(top, mix_b[...])) * 256.0 + dot(rest, mix_a[...])
        score = mixed * SCORE_STEP
        peak = jnp.max(jnp.where(alive, score, -512.0), axis=0, keepdims=True)
        peak = jnp.ceil(peak)
        weights[0:rows, g * w : (g + 1) * w] = jnp.where(alive, jnp.exp2(score - peak), 0.0).astype(BF)
        weights[rows:, g * w : (g + 1) * w] = jnp.broadcast_to(peak, (TILE, w)).astype(BF)
    for k in range(nl):
        outs[k][...] = weights[:, lanes_at((loc ^ k) * plan.states, plan.states)]


def mass_kernel(plan, at, mass, hit, second, *refs):
    outs, (held,) = refs[: plan.n_inc], refs[plan.n_inc :]
    inc, w = at[1], plan.wide
    for t in range(plan.n_inc):
        x = mass[:, t * w : (t + 1) * w]
        top = x.astype(BF)
        rest = (x - top.astype(F32)).astype(BF)
        moved = (dot(top, hit[t]) + dot(rest, hit[t])).astype(BF)
        for q in range(plan.n_inc):
            held[q, :, t * LANES : (t + 1) * LANES] = moved[:, q * LANES : (q + 1) * LANES]
    for k in range(plan.n_inc):
        outs[k][...] = dot(held[inc ^ k], second[...]).astype(BF)


def spread_kernel(plan, at, *refs):
    ni, nl = plan.n_inc, plan.n_loc
    ins, outs, (held,) = refs[:ni], refs[ni : ni + nl], refs[ni + nl :]
    loc, inc = at[0], at[1]
    for k in range(ni):
        for g in range(plan.groups):
            held[:, lanes_at(g * plan.wide + (inc ^ k) * LANES, LANES)] = ins[k][
                :, g * LANES : (g + 1) * LANES
            ]
    for k in range(nl):
        outs[k][...] = held[:, lanes_at((loc ^ k) * plan.states, plan.states)]


def collect_kernel(plan, at, *refs):
    ni, nl = plan.n_inc, plan.n_loc
    ins, outs, (held,) = refs[:nl], refs[nl : nl + ni], refs[nl + ni :]
    loc, inc = at[0], at[1]
    for k in range(nl):
        held[:, lanes_at((loc ^ k) * plan.states, plan.states)] = ins[k][...]
    for k in range(ni):
        for g in range(plan.groups):
            outs[k][:, g * LANES : (g + 1) * LANES] = held[
                :, lanes_at(g * plan.wide + (inc ^ k) * LANES, LANES)
            ]


def window_kernel(plan, at, cost, outs, quarter, held):
    loc, inc, n = at[0], at[1], plan.counties
    near = jnp.exp(-cost[...]).astype(BF)
    held[:, :n] = near
    held[:, n:] = near[:, : plan.window - LANES]
    step = TILE
    for g in range(plan.rows // step):
        block = (loc * plan.rows + g * step) // LANES
        outs[g * step : (g + 1) * step, :] = held[
            g * step : (g + 1) * step, lanes_at(block * LANES, plan.window)
        ]
    quarter[...] = outs[pl.ds(pl.multiple_of(inc * plan.stride, TILE), plan.quarter), :]


def solve_kernel(plan, at, *refs):
    nl, ni, rows, n = plan.n_loc, plan.n_inc, plan.rows, plan.counties
    weights, masses, pieces, refs = refs[:nl], refs[nl : 2 * nl], refs[2 * nl], refs[2 * nl + 1 :]
    totals, movers, refs = refs[:nl], refs[nl : 2 * nl], refs[2 * nl :]
    strip, full, weight, share, sums, sem = refs
    loc = at[0]
    copies = []
    for p in range(nl):
        for q in range(ni):
            size = plan.stride if q < ni - 1 else plan.quarter
            start = p * rows + q * plan.stride
            copies.append(
                pltpu.make_async_copy(
                    pieces.at[p * ni + q, pl.ds(0, size)], strip.at[pl.ds(start, size)], sem
                )
            )
    for c in copies:
        c.start()

    peak = weights[0][rows : rows + 1, :].astype(F32)
    for k in range(1, nl):
        peak = jnp.maximum(peak, weights[k][rows : rows + 1, :].astype(F32))
    for k in range(nl):
        scale = jnp.exp2(weights[k][rows : rows + 1, :].astype(F32) - peak)
        at_rows = pl.ds(pl.multiple_of((loc ^ k) * rows, TILE), rows)
        weight[at_rows, :] = (weights[k][:rows, :].astype(F32) * scale).astype(BF)

    for c in copies:
        c.wait()
    blocks = plan.block_rows
    for i in range(blocks):
        for k in range(plan.window // LANES):
            j = (i + k) % blocks
            tile = strip[i * LANES : (i + 1) * LANES, k * LANES : (k + 1) * LANES]
            full[i * LANES : (i + 1) * LANES, j * LANES : (j + 1) * LANES] = tile
            if k:
                full[j * LANES : (j + 1) * LANES, i * LANES : (i + 1) * LANES] = tile.T

    chunk = LANES * (5 if blocks % 5 == 0 else 1)

    def first(i, carry):
        r = pl.ds(pl.multiple_of(i * chunk, LANES), chunk)
        sums[r, :] = dot(full[r, :], weight[...])
        return carry

    lax.fori_loop(0, n // chunk, first, 0)
    for k in range(nl):
        r = pl.ds(pl.multiple_of((loc ^ k) * rows, TILE), rows)
        total = sums[r, :]
        totals[k][:rows, :] = total.astype(BF)
        totals[k][rows:, :] = jnp.broadcast_to(peak, (TILE, plan.states)).astype(BF)
        share[r, :] = (masses[k][...].astype(F32) / total).astype(BF)

    def second(i, carry):
        r = pl.ds(pl.multiple_of(i * chunk, LANES), chunk)
        sums[r, :] = dot(full[r, :], share[...])
        return carry

    lax.fori_loop(0, n // chunk, second, 0)
    for k in range(nl):
        r = pl.ds(pl.multiple_of((loc ^ k) * rows, TILE), rows)
        movers[k][...] = (weight[r, :].astype(F32) * sums[r, :]).astype(BF)


def tail_kernel(plan, at, *refs):
    ni, nl = plan.n_inc, plan.n_loc
    ins, (mix_a, mix_b), refs = refs[:nl], refs[nl : nl + 2], refs[nl + 2 :]
    outs, (held, mixed) = refs[:ni], refs[ni:]
    loc, inc, w = at[0], at[1], plan.wide
    for k in range(nl):
        held[:, lanes_at((loc ^ k) * plan.states, plan.states)] = ins[k][...]
    for g in range(plan.groups):
        x = held[:, g * w : (g + 1) * w]
        mixed[...] = (dot_nt(x, mix_a[...]) + dot_nt(x, mix_b[...])).astype(BF)
        for k in range(ni):
            outs[k][:, g * LANES : (g + 1) * LANES] = mixed[:, lanes_at((inc ^ k) * LANES, LANES)]


def restore(plan, inc, ins, second, held):
    for k in range(plan.n_inc):
        back = dot_nt(ins[k][...], second[...]).astype(BF)
        for t in range(plan.n_inc):
            held[t, :, lanes_at((inc ^ k) * LANES, LANES)] = back[:, t * LANES : (t + 1) * LANES]


def next_mass_kernel(plan, at, *refs):
    ni, w = plan.n_inc, plan.wide
    ins, (first, second), (out, held) = refs[:ni], refs[ni : ni + 2], refs[ni + 2 :]
    restore(plan, at[1], ins, second, held)
    for t in range(ni):
        out[:, t * w : (t + 1) * w] = dot_nt(held[t], first[...])


def value_kernel(plan, at, *refs):
    ni, w, rows = plan.n_inc, plan.wide, plan.rows
    ins, (hit, second, flow), (out, held) = refs[:ni], refs[ni : ni + 3], refs[ni + 3 :]
    restore(plan, at[1], ins, second, held)
    for t in range(ni):
        got = dot_nt(held[t], hit[t])
        peak = got[rows : rows + 1, :] * LN2 + SCORE_SHIFT
        out[:, t * w : (t + 1) * w] = flow[:, t * w : (t + 1) * w] + (peak + jnp.log(got[:rows, :]))


def mix_maps(plan, trans_weight):
    e = plan.incomes
    raised = trans_weight + 16.0 * jnp.eye(e, dtype=F32)
    prob = raised / jnp.sum(raised, axis=1, keepdims=True)
    ni, oi, ga = plan.n_inc, plan.own_incomes, plan.group_assets
    turned = prob.T.reshape(ni, 1, oi, ni, 1, oi)
    grid = jnp.broadcast_to(turned, (ni, ga, oi, ni, ga, oi)).reshape(plan.wide, plan.wide)
    r = lax.broadcasted_iota(jnp.int32, grid.shape, 0) // oi % ga
    c = lax.broadcasted_iota(jnp.int32, grid.shape, 1) // oi % ga
    grid = jnp.where(r == c, grid, 0.0)
    top = lax.reduce_precision(grid, 8, 7)
    return top.astype(BF), (grid - top).astype(BF)


def policy_maps(plan, asset_policy, inc):
    ni, oa, a, w = plan.n_inc, plan.own_assets, plan.assets, plan.wide
    own = lax.dynamic_slice_in_dim(asset_policy, inc * plan.own_incomes, plan.own_incomes, 0)
    group = w // a
    row_income = jnp.arange(group, dtype=jnp.int32)[None, :, None]
    own = own.reshape(ni, group, a)
    lane = own // oa * LANES + row_income * oa + own % oa
    lane = lane.reshape(ni, w, 1)
    return (lane == lax.broadcasted_iota(jnp.int32, (ni, w, w), 2)).astype(BF)


def swap(x, axis, n, k):
    if k == 0:
        return x
    return lax.ppermute(x, axis, [(s, s ^ k) for s in range(n)])


def far_first(n):
    return sorted(range(1, n), key=lambda k: -k)


def exchange(blocks, axis, n):
    got = {0: blocks[0]}
    for k in far_first(n):
        got[k] = swap(blocks[k], axis, n, k)
    return [got[k] for k in range(n)]


def state_split(plan, cont_value, flow_util, move_cost, live_mask, trans_weight, asset_policy, mass):
    ni, nl, rows, n = plan.n_inc, plan.n_loc, plan.rows, plan.counties
    w, part, states, packed = plan.wide, plan.part, plan.states, plan.packed
    S = jax.ShapeDtypeStruct
    loc, inc = lax.axis_index("loc"), lax.axis_index("inc")
    at = jnp.stack([loc, inc]).astype(jnp.int32)
    bind = lambda f: functools.partial(f, plan)
    pass_flops = 2 * rows * plan.columns * w

    first, second = order_maps(plan)
    codes = call(
        bind(encode_kernel),
        [S((rows, part), jnp.int16)] * ni,
        [at, cont_value, first, second],
        [pltpu.VMEM((ni, rows, w), BF)] * 2,
        4 * pass_flops,
    )
    codes = exchange(codes, "inc", ni)

    _, quarter = call(
        bind(window_kernel),
        [S((rows, plan.window), BF), S((plan.quarter, plan.window), BF)],
        [at, move_cost],
        [pltpu.VMEM((rows, n + plan.window - LANES), BF)],
    )
    pieces = lax.all_gather(quarter, ("loc", "inc"), axis=0)

    hit = policy_maps(plan, asset_policy, inc)
    masses = call(
        bind(mass_kernel),
        [S((rows, part), BF)] * ni,
        [at, mass, hit, second],
        [pltpu.VMEM((ni, rows, w), BF)],
        3 * pass_flops,
    )
    masses = exchange(masses, "inc", ni)
    masses = call(
        bind(spread_kernel),
        [S((rows, states), BF)] * nl,
        [at, *masses],
        [pltpu.VMEM((rows, plan.columns), BF)],
    )

    mix_a, mix_b = mix_maps(plan, trans_weight)
    live = (live_mask > 0).astype(F32)[:, None]
    weights = call(
        bind(weight_kernel),
        [S((packed, states), BF)] * nl,
        [at, *codes, mix_a, mix_b, live],
        [pltpu.VMEM((rows, w), jnp.int32), pltpu.VMEM((packed, plan.columns), BF)],
        3 * pass_flops,
    )
    weights = exchange(weights, "loc", nl)
    masses = exchange(masses, "loc", nl)

    out = call(
        bind(solve_kernel),
        [S((packed, states), BF)] * nl + [S((rows, states), BF)] * nl,
        [at, *weights, *masses, pieces],
        [
            pltpu.VMEM((n, plan.window), BF),
            pltpu.VMEM((n, n), BF),
            pltpu.VMEM((n, states), BF),
            pltpu.VMEM((n, states), BF),
            pltpu.VMEM((n, states), F32),
            pltpu.SemaphoreType.DMA,
        ],
        4 * n * n * states,
        [SMEM] + [VMEM] * (2 * nl) + [ANY],
        60,
    )
    totals, movers = out[:nl], out[nl:]
    movers = exchange(movers, "loc", nl)
    totals = exchange(totals, "loc", nl)

    moved = call(
        bind(tail_kernel),
        [S((rows, part), BF)] * ni,
        [at, *movers, mix_a, mix_b],
        [pltpu.VMEM((rows, plan.columns), BF), pltpu.VMEM((rows, w), BF)],
        2 * pass_flops,
    )
    moved = exchange(moved, "inc", ni)
    totals = call(
        bind(collect_kernel),
        [S((packed, part), BF)] * ni,
        [at, *totals],
        [pltpu.VMEM((packed, plan.columns), BF)],
    )
    totals = exchange(totals, "inc", ni)

    (new_mass,) = call(
        bind(next_mass_kernel),
        [S((rows, plan.columns), F32)],
        [at, *moved, first, second],
        [pltpu.VMEM((ni, rows, w), BF)],
        2 * pass_flops,
    )
    (new_value,) = call(
        bind(value_kernel),
        [S((rows, plan.columns), F32)],
        [at, *totals, hit, second, flow_util],
        [pltpu.VMEM((ni, packed, w), BF)],
        2 * pass_flops,
    )
    return new_value, new_mass


def gathered(cont_value, flow_util, move_cost, live_mask, trans_weight, asset_policy, mass):
    high = lax.Precision.HIGHEST
    e, a = asset_policy.shape
    raised = trans_weight + 16.0 * jnp.eye(e, dtype=F32)
    trans_prob = raised / jnp.sum(raised, axis=1, keepdims=True)
    onehot = (asset_policy[:, :, None] == jnp.arange(a, dtype=jnp.int32)[None, None, :]).astype(F32)
    moved_rows = lax.all_to_all(cont_value, "inc", split_axis=0, concat_axis=1, tiled=True)
    expect = jnp.einsum("ef,jfb->jeb", trans_prob, moved_rows.reshape(-1, e, a), precision=high)
    chosen_all = jnp.einsum("jeb,eab->jea", expect, onehot, precision=high).reshape(-1, e * a)
    chosen = lax.all_to_all(chosen_all, "inc", split_axis=1, concat_axis=0, tiled=True)
    scores = DISCOUNT * chosen
    live_rows = live_mask[:, None] > 0
    local_max = jnp.max(jnp.where(live_rows, scores, F32(-1e30)), axis=0)
    column_max = lax.pmax(local_max, "loc")
    dest_weight = jnp.where(live_rows, jnp.exp(scores - column_max[None, :]), F32(0.0)).astype(BF)
    kernel = jnp.exp(-move_cost).astype(BF)
    totals = dot(kernel, lax.all_gather(dest_weight, "loc", axis=0, tiled=True))
    new_value = flow_util + column_max[None, :] + jnp.log(totals)
    shares = (mass / totals).astype(BF)
    arrived = lax.psum_scatter(
        lax.dot_general(
            kernel, shares, (((0,), (0,)), ((), ())), preferred_element_type=F32
        ).astype(BF),
        "loc",
        scatter_dimension=0,
        tiled=True,
    ).astype(F32)
    movers = dest_weight.astype(F32) * arrived
    moved_mass = lax.all_to_all(movers, "inc", split_axis=0, concat_axis=1, tiled=True)
    shuffled = jnp.einsum("jea,eab->jeb", moved_mass.reshape(-1, e, a), onehot, precision=high)
    mixed_mass = jnp.einsum("ef,jeb->jfb", trans_prob, shuffled, precision=high).reshape(-1, e * a)
    new_mass = lax.all_to_all(mixed_mass, "inc", split_axis=1, concat_axis=0, tiled=True)
    return new_value, new_mass


def solution(mesh):
    n_loc, n_inc = mesh.shape["loc"], mesh.shape["inc"]

    def shards(*args):
        rows, columns = args[0].shape
        plan = Plan(n_loc, n_inc, args[2].shape[1], rows, columns, *args[5].shape)
        if plan.fits():
            return state_split(plan, *args)
        return gathered(*args)

    split = P("loc", "inc")
    return jax.shard_map(
        shards,
        mesh=mesh,
        in_specs=(split, split, P("loc", None), P("loc"), P(), P(), split),
        out_specs=(split, split),
        check_vma=False,
    )
```

```python
import functools
import math

import jax
import jax.numpy as jnp
from jax import lax
from jax.experimental import pallas as pl
from jax.experimental.pallas import tpu as pltpu
from jax.sharding import PartitionSpec as P

DISCOUNT = 0.96
LANES = 128
TILE = 16
VALUE_LOW = -4.0
VALUE_HIGH = 252.0
STEP = (VALUE_HIGH - VALUE_LOW) / 65535.0
HALF = 32768.0
LN2 = math.log(2.0)
SCORE_STEP = DISCOUNT * STEP / LN2
SCORE_SHIFT = DISCOUNT * (HALF * STEP + VALUE_LOW)

BF = jnp.bfloat16
F32 = jnp.float32
VMEM = pl.BlockSpec(memory_space=pltpu.VMEM)
SMEM = pl.BlockSpec(memory_space=pltpu.SMEM)
ANY = pl.BlockSpec(memory_space=pl.ANY)


def dot(a, b):
    return lax.dot_general(a, b, (((1,), (0,)), ((), ())), preferred_element_type=F32)


def dot_nt(a, b):
    return lax.dot_general(a, b, (((1,), (1,)), ((), ())), preferred_element_type=F32)


def lanes_at(start, size):
    return pl.ds(pl.multiple_of(start, LANES), size)


def call(kernel, outs, ins, scratch=(), flops=0, specs=None, out_specs=None, vmem=48):
    moved = sum(math.prod(x.shape) * x.dtype.itemsize for x in list(ins) + list(outs))
    return pl.pallas_call(
        kernel,
        out_shape=tuple(outs),
        in_specs=specs or [SMEM] + [VMEM] * (len(ins) - 1),
        out_specs=tuple(out_specs or [VMEM] * len(outs)),
        scratch_shapes=list(scratch),
        compiler_params=pltpu.CompilerParams(vmem_limit_bytes=vmem * 1024 * 1024),
        cost_estimate=pl.CostEstimate(flops=flops, bytes_accessed=moved, transcendentals=0),
    )(*ins)


class Plan:
    def __init__(self, n_loc, n_inc, counties, rows, columns, incomes, assets):
        self.n_loc, self.n_inc, self.n_z = n_loc, n_inc, n_loc // 2
        self.counties, self.rows, self.columns = counties, rows, columns
        self.incomes, self.assets = incomes, assets
        self.own_incomes = incomes // n_inc
        self.own_assets = assets // n_inc
        self.group_assets = LANES // self.own_incomes
        self.wide = n_inc * LANES
        self.packed = rows + TILE
        self.half = counties // 2
        self.block_rows = counties // LANES
        self.window = (self.block_rows // 2 + 1) * LANES
        self.stride = rows // n_inc // TILE * TILE
        self.quarter = rows - self.stride * (n_inc - 1)
        self.cut = (self.window // LANES + 1) // 2 * LANES

    def fits(self):
        power = lambda n: n > 1 and n & (n - 1) == 0
        return (
            power(self.n_loc)
            and power(self.n_z)
            and power(self.n_inc)
            and self.incomes == LANES
            and self.own_incomes * self.group_assets == LANES
            and self.columns == self.n_z * self.wide
            and self.n_z == self.n_inc == 4
            and self.own_assets == self.n_z * self.group_assets
            and self.rows % TILE == 0
            and self.counties == self.rows * self.n_loc
            and self.counties % LANES == 0
            and self.block_rows % 2 == 1
        )


def order_maps(plan):
    w, oa, oi = plan.wide, plan.own_assets, plan.own_incomes
    r = lax.broadcasted_iota(jnp.int32, (w, w), 0)
    c = lax.broadcasted_iota(jnp.int32, (w, w), 1)
    a = plan.assets
    spot = (r % a) // oa * LANES + r // a * oa + r % oa
    first = (c == spot).astype(BF)
    second = (c == r % oa * oi + r // oa).astype(BF)
    return first, second


def encode_kernel(plan, at, value, first, second, *refs):
    outs, (high, low) = refs[: plan.n_inc], refs[plan.n_inc :]
    inc, w = at[1], plan.wide
    for t in range(plan.n_inc):
        x = value[:, t * w : (t + 1) * w]
        code = jnp.clip(jnp.round((x - VALUE_LOW) * (1.0 / STEP)) - HALF, -HALF, HALF - 1.0)
        top = jnp.floor(code * (1.0 / 256.0))
        rest = code - 256.0 * top
        moved_top = dot(top.astype(BF), first[...]).astype(BF)
        moved_rest = dot(rest.astype(BF), first[...]).astype(BF)
        for q in range(plan.n_inc):
            high[q, :, t * LANES : (t + 1) * LANES] = moved_top[:, q * LANES : (q + 1) * LANES]
            low[q, :, t * LANES : (t + 1) * LANES] = moved_rest[:, q * LANES : (q + 1) * LANES]
    for k in range(plan.n_inc):
        q = inc ^ k
        code = dot(high[q], second[...]) * 256.0 + dot(low[q], second[...])
        outs[k][...] = code.astype(jnp.int32).astype(jnp.int16)


def weight_kernel(plan, at, *refs):
    ni, nz, rows = plan.n_inc, plan.n_z, plan.rows
    codes, (mix_a, mix_b, live), refs = refs[:ni], refs[ni : ni + 3], refs[ni + 3 :]
    weights, held = refs
    inc, w = at[1], plan.wide
    alive = live[...] > 0.0
    for g in range(nz):
        for k in range(ni):
            held[:, lanes_at((inc ^ k) * LANES, LANES)] = codes[k][
                :, g * LANES : (g + 1) * LANES
            ].astype(jnp.int32)
        code = held[...]
        top = (code >> 8).astype(F32).astype(BF)
        rest = (code & 255).astype(F32).astype(BF)
        mixed = (dot(top, mix_a[...]) + dot(top, mix_b[...])) * 256.0 + dot(rest, mix_a[...])
        score = mixed * SCORE_STEP
        peak = jnp.max(jnp.where(alive, score, -512.0), axis=0, keepdims=True)
        peak = jnp.ceil(peak)
        weights[g, 0:rows, :] = jnp.where(alive, jnp.exp2(score - peak), 0.0).astype(BF)
        weights[g, rows:, :] = jnp.broadcast_to(peak, (TILE, w)).astype(BF)


def mass_kernel(plan, at, mass, hit, second, *refs):
    outs, (held,) = refs[: plan.n_inc], refs[plan.n_inc :]
    inc, w = at[1], plan.wide
    for t in range(plan.n_inc):
        x = mass[:, t * w : (t + 1) * w]
        top = x.astype(BF)
        rest = (x - top.astype(F32)).astype(BF)
        moved = (dot(top, hit[t]) + dot(rest, hit[t])).astype(BF)
        for q in range(plan.n_inc):
            held[q, :, t * LANES : (t + 1) * LANES] = moved[:, q * LANES : (q + 1) * LANES]
    for k in range(plan.n_inc):
        outs[k][...] = dot(held[inc ^ k], second[...]).astype(BF)


def spread_kernel(plan, at, *refs):
    *ins, out = refs
    for k in range(plan.n_inc):
        for g in range(plan.n_z):
            out[g, :, lanes_at((at[1] ^ k) * LANES, LANES)] = ins[k][
                :, g * LANES : (g + 1) * LANES
            ]


def collect_kernel(plan, at, *refs):
    blocks, *outs = refs
    for k in range(plan.n_inc):
        for g in range(plan.n_z):
            outs[k][:, g * LANES : (g + 1) * LANES] = blocks[
                g, :, lanes_at((at[1] ^ k) * LANES, LANES)
            ]


def windows(plan, start, count, near, held, out):
    n = plan.counties
    held[:, :n] = near
    held[:, n:] = near[:, : plan.window - LANES]
    for g in range(count // TILE):
        block = (start + g * TILE) // LANES
        out[g * TILE : (g + 1) * TILE, :] = held[
            g * TILE : (g + 1) * TILE, lanes_at(block * LANES, plan.window)
        ]


def quarter_kernel(plan, at, cost, out, part, held, sem):
    start = pl.multiple_of(at[1] * plan.stride, TILE)
    copy = pltpu.make_async_copy(cost.at[pl.ds(start, plan.quarter)], part, sem)
    copy.start()
    copy.wait()
    near = jnp.exp(-part[...]).astype(BF)
    windows(plan, at[0] * plan.rows + start, plan.quarter, near, held, out)


def window_kernel(plan, at, cost, out, held):
    near = jnp.exp(-cost[...]).astype(BF)
    windows(plan, at[0] * plan.rows, plan.rows, near, held, out)


def county_rows(plan, at, z, side):
    start = (2 * z + ((at[0] % 2) ^ side)) * plan.rows
    return pl.ds(pl.multiple_of(start, TILE), plan.rows)


def near_copies(plan, near, held, sems):
    blocks = [pl.ds(j * plan.rows, plan.rows) for j in range(plan.n_z)]
    return [
        pltpu.make_async_copy(near.at[b], held.at[b], sems.at[j]) for j, b in enumerate(blocks)
    ]


def total_kernel(plan, at, *refs):
    nz, rows, cut = plan.n_z, plan.rows, plan.cut
    own_weights, other_weights, refs = refs[0], refs[1], refs[2:]
    both, (sent, scaled, near, weight, strip, full, sums, sem) = refs[:10], refs[10:]
    z, core, inc = at[0] // 2, at[0] % 2, at[1]
    left, right = pl.ds(0, cut), pl.ds(cut, plan.window - cut)
    always, last = [], []
    for side in range(2):
        own, *parts = both[side * 5 : side * 5 + 5]
        first_row = lambda j: (2 * (z ^ j) + (core ^ side)) * rows
        always.append((own, strip.at[pl.ds(pl.multiple_of(first_row(0), TILE), rows)]))
        places = ((0, 1), left), ((2, 3), left), ((0, 2), right), ((1, 3), right)
        for part, (steps, lanes) in zip(parts, places):
            for h, k in enumerate(steps):
                q = inc ^ k
                for j in range(1, nz):
                    base = (h * (nz - 1) + j - 1) * plan.quarter
                    start = first_row(j) + q * plan.stride
                    rest = plan.quarter - plan.stride
                    to = lambda r, size: strip.at[pl.ds(pl.multiple_of(r, TILE), size), lanes]
                    always.append((part.at[pl.ds(base, plan.stride)], to(start, plan.stride)))
                    extra = part.at[pl.ds(base + plan.stride, rest)]
                    last.append((q == plan.n_inc - 1, extra, to(start + plan.stride, rest)))
    copies = [pltpu.make_async_copy(a, b, sem) for a, b in always]
    more = [(c, pltpu.make_async_copy(a, b, sem)) for c, a, b in last]
    for c in copies:
        c.start()
    for when, c in more:
        pl.when(when)(c.start)

    places = [(x, g) for x in (own_weights, other_weights) for g in range(nz)]
    peaks = [x[g, rows : rows + 1, :].astype(F32) for x, g in places]
    peak = functools.reduce(jnp.maximum, peaks)
    for i, (x, g) in enumerate(places):
        part = (x[g, :rows, :].astype(F32) * jnp.exp2(peaks[i] - peak)).astype(BF)
        weight[county_rows(plan, at, g, i // nz), :] = part
        if i < nz:
            scaled[g] = part

    for c in copies:
        c.wait()
    for when, c in more:
        pl.when(when)(c.wait)
    blocks = plan.block_rows
    for i in range(blocks):
        for k in range(plan.window // LANES):
            j = (i + k) % blocks
            tile = strip[i * LANES : (i + 1) * LANES, k * LANES : (k + 1) * LANES]
            full[i * LANES : (i + 1) * LANES, j * LANES : (j + 1) * LANES] = tile
            if k:
                full[j * LANES : (j + 1) * LANES, i * LANES : (i + 1) * LANES] = tile.T
    copies = []
    for j in range(nz):
        out = near.at[pl.ds(j * rows, rows)]
        copies.append(pltpu.make_async_copy(full.at[county_rows(plan, at, j, 0)], out, sem))
    for c in copies:
        c.start()
    def product(j, carry):
        sums[j] = dot(full[county_rows(plan, at, j, 0), :], weight[...])
        return carry

    lax.fori_loop(0, nz, product, 0)
    sent[:, :rows, :] = sums[...].astype(BF)
    sent[:, rows:, :] = jnp.broadcast_to(peak[None], (nz, TILE, plan.wide)).astype(BF)
    for c in copies:
        c.wait()


def share_kernel(plan, masses, totals, out):
    for g in range(plan.n_z):
        total = totals[g, : plan.rows, :].astype(F32)
        out[g] = (masses[g].astype(F32) / total).astype(BF)


def mover_kernel(plan, at, own, other, near, scaled, *refs):
    nz, rows = plan.n_z, plan.rows
    outs, (movers, share, held, sems) = refs[:nz], refs[nz:]
    copies = near_copies(plan, near, held, sems)
    for c in copies:
        c.start()
    for side, x in enumerate((own, other)):
        for g in range(nz):
            share[county_rows(plan, at, g, side), :] = x[g]
    for g in range(nz):
        copies[g].wait()
        arrived = dot(held[g * rows : (g + 1) * rows, :], share[...])
        movers[g] = (scaled[g].astype(F32) * arrived).astype(BF)
    for j in range(nz):
        outs[j][...] = movers[(at[0] // 2) ^ j]


def tail_kernel(plan, at, *refs):
    ni, rows, w = plan.n_inc, plan.rows, plan.wide
    mix_a, mix_b, *refs = refs
    ins, outs, mixed = refs[: -1 - ni], refs[-1 - ni : -1], refs[-1]
    for i, part in enumerate(ins):
        x = part[...]
        new = dot_nt(x, mix_a[...]) + dot_nt(x, mix_b[...])
        most = jnp.maximum(jnp.max(new, axis=0, keepdims=True), 1e-30)
        power = jnp.ceil(jnp.log2(most))
        code = jnp.minimum(jnp.round(new * jnp.exp2(15.0 - power)), HALF - 1.0)
        mixed[:rows, :] = code.astype(jnp.int32)
        mixed[rows:, :] = jnp.broadcast_to(power, (TILE, w)).astype(jnp.int32)
        for k in range(ni):
            outs[k][:, i * LANES : (i + 1) * LANES] = mixed[
                :, lanes_at((at[1] ^ k) * LANES, LANES)
            ].astype(jnp.int16)


def next_mass_kernel(plan, at, *refs):
    ni, w, rows = plan.n_inc, plan.wide, plan.rows
    close, far, refs = refs[:ni], refs[ni : 2 * ni], refs[2 * ni :]
    first, second, out, held, high, low = refs
    z, inc = at[0] // 2, at[1]
    for k in range(ni):
        j = 0
        for part in (close[k], far[k]):
            for i in range(part.shape[1] // LANES):
                held[:, lanes_at((z ^ j) * LANES, LANES)] = part[
                    :, i * LANES : (i + 1) * LANES
                ].astype(jnp.int32)
                j += 1
        code = held[...]
        for part, into in ((code >> 8, high), (code & 255, low)):
            back = dot_nt(part.astype(F32).astype(BF), second[...]).astype(BF)
            for t in range(ni):
                into[t, :, lanes_at((inc ^ k) * LANES, LANES)] = back[:, t * LANES : (t + 1) * LANES]
    for t in range(ni):
        code = dot_nt(high[t], first[...]) * 256.0 + dot_nt(low[t], first[...])
        out[:, t * w : (t + 1) * w] = code[:rows, :] * jnp.exp2(code[rows : rows + 1, :] - 15.0)


def value_kernel(plan, at, *refs):
    ni, w, rows = plan.n_inc, plan.wide, plan.rows
    ins, (hit, second, flow), (out, held) = refs[:ni], refs[ni : ni + 3], refs[ni + 3 :]
    inc = at[1]
    for k in range(ni):
        back = dot_nt(ins[k][...], second[...]).astype(BF)
        for t in range(ni):
            held[t, :, lanes_at((inc ^ k) * LANES, LANES)] = back[:, t * LANES : (t + 1) * LANES]
    for t in range(ni):
        got = dot_nt(held[t], hit[t])
        peak = got[rows : rows + 1, :] * LN2 + SCORE_SHIFT
        out[:, t * w : (t + 1) * w] = flow[:, t * w : (t + 1) * w] + (peak + jnp.log(got[:rows, :]))


def mix_kernel(plan, trans, out_a, out_b):
    e, oi, ga, w = plan.incomes, plan.own_incomes, plan.group_assets, plan.wide
    grid = lambda shape, axis: lax.broadcasted_iota(jnp.int32, shape, axis)
    raised = trans[...] + jnp.where(grid((e, e), 0) == grid((e, e), 1), 16.0, 0.0)
    prob = (raised / jnp.sum(raised, axis=1, keepdims=True)).T
    lane = grid((e, w), 1)
    place = (grid((e, w), 0) == lane // LANES * oi + lane % oi).astype(BF)
    same = grid((w, w), 0) // oi % ga == grid((w, w), 1) // oi % ga
    top = prob.astype(BF)
    for part, out in ((top, out_a), ((prob - top.astype(F32)).astype(BF), out_b)):
        wide = dot(part, place)
        blocks = [wide[i * oi : (i + 1) * oi] for i in range(plan.n_inc) for _ in range(ga)]
        out[...] = jnp.where(same, jnp.concatenate(blocks, axis=0), 0.0).astype(BF)


def policy_maps(plan, asset_policy, inc):
    ni, oa, a, w = plan.n_inc, plan.own_assets, plan.assets, plan.wide
    own = lax.dynamic_slice_in_dim(asset_policy, inc * plan.own_incomes, plan.own_incomes, 0)
    group = w // a
    row_income = jnp.arange(group, dtype=jnp.int32)[None, :, None]
    own = own.reshape(ni, group, a)
    lane = own // oa * LANES + row_income * oa + own % oa
    lane = lane.reshape(ni, w, 1)
    return (lane == lax.broadcasted_iota(jnp.int32, (ni, w, w), 2)).astype(BF)


def swap(x, axis, n, k):
    return lax.ppermute(x, axis, [(s, s ^ k) for s in range(n)]) if k else x


def exchange(blocks, axis, n, unit=1):
    got = {k: swap(blocks[k], axis, n, k * unit) for k in reversed(range(len(blocks)))}
    return [got[k] for k in range(len(blocks))]


def after(x, y):
    return lax.optimization_barrier((x, y))


def state_split(plan, cont_value, flow_util, move_cost, live_mask, trans_weight, asset_policy, mass):
    ni, nl, nz, rows, n = plan.n_inc, plan.n_loc, plan.n_z, plan.rows, plan.counties
    w, packed, half = plan.wide, plan.packed, plan.half
    S = jax.ShapeDtypeStruct
    loc, inc = lax.axis_index("loc"), lax.axis_index("inc")
    at = jnp.stack([loc, inc]).astype(jnp.int32)
    bind = lambda f: functools.partial(f, plan)
    pass_flops = 2 * rows * plan.columns * w
    solve_flops = 2 * half * n * w
    swap_core = lambda x: swap(x, "loc", nl, 1)
    lines = [list(range(core, nl, 2)) for core in range(2)]
    along_z = lambda x: lax.all_to_all(x, "loc", 0, 0, axis_index_groups=lines)
    ring = n + plan.window - LANES

    (quarter,) = call(
        bind(quarter_kernel),
        [S((plan.quarter, plan.window), BF)],
        [at, move_cost],
        [
            pltpu.VMEM((plan.quarter, n), F32),
            pltpu.VMEM((plan.quarter, ring), BF),
            pltpu.SemaphoreType.DMA,
        ],
        specs=[SMEM, ANY],
    )
    pieces = [swap(quarter, "loc", nl, 2 * j) for j in range(2, nz)]

    first, second = order_maps(plan)
    codes = call(
        bind(encode_kernel),
        [S((rows, w), jnp.int16)] * ni,
        [at, cont_value, first, second],
        [pltpu.VMEM((ni, rows, w), BF)] * 2,
        4 * pass_flops,
    )
    codes = exchange(codes, "inc", ni)
    quarter, _ = after(quarter, codes[1])
    pieces.insert(0, swap(quarter, "loc", nl, 2))

    hit = policy_maps(plan, asset_policy, inc)
    masses = call(
        bind(mass_kernel),
        [S((rows, w), BF)] * ni,
        [at, mass, hit, second],
        [pltpu.VMEM((ni, rows, w), BF)],
        3 * pass_flops,
    )
    mix_a, mix_b = call(
        bind(mix_kernel), [S((w, w), BF)] * 2, [trans_weight], specs=[VMEM]
    )
    (own_near,) = call(
        bind(window_kernel),
        [S((rows, plan.window), BF)],
        [at, move_cost],
        [pltpu.VMEM((rows, ring), BF)],
    )
    masses, codes = after(masses, codes)
    masses = exchange(masses, "inc", ni)
    codes, _ = after(codes, pieces)

    live = (live_mask > 0).astype(F32)[:, None]
    weights = call(
        bind(weight_kernel),
        [S((nz, packed, w), BF)],
        [at, *codes, mix_a, mix_b, live],
        [pltpu.VMEM((rows, w), jnp.int32)],
        3 * pass_flops,
    )
    weights = along_z(weights[0])
    others = swap_core(weights)

    strip, _ = after(jnp.concatenate(pieces), masses)
    left, right = strip[:, : plan.cut], strip[:, plan.cut :]
    left = jnp.concatenate([left, swap(left, "inc", ni, 1)])
    right = jnp.concatenate([right, swap(right, "inc", ni, 2)])
    near = [own_near, left, swap(left, "inc", ni, 2), right, swap(right, "inc", ni, 1)]
    near = near + [swap_core(x) for x in near]

    masses = call(bind(spread_kernel), [S((nz, rows, w), BF)], [at, *masses])
    masses, weights = after(masses[0], weights)
    masses = along_z(masses)

    totals, scaled, near = call(
        bind(total_kernel),
        [S((nz, packed, w), BF), S((nz, rows, w), BF), S((half, n), BF)],
        [at, weights, others, *near],
        [
            pltpu.VMEM((n, w), BF),
            pltpu.VMEM((n, plan.window), BF),
            pltpu.VMEM((n, n), BF),
            pltpu.VMEM((nz, rows, w), F32),
            pltpu.SemaphoreType.DMA,
        ],
        solve_flops,
        specs=[SMEM, VMEM, VMEM] + [ANY] * len(near),
        out_specs=[VMEM, VMEM, ANY],
        vmem=60,
    )
    sent = along_z(totals)
    (share,) = call(
        bind(share_kernel), [S((nz, rows, w), BF)], [masses, totals], specs=[VMEM] * 2
    )
    movers = call(
        bind(mover_kernel),
        [S((rows, w), BF)] * nz,
        [at, share, swap_core(share), near, scaled],
        [
            pltpu.VMEM((nz, rows, w), BF),
            pltpu.VMEM((n, w), BF),
            pltpu.VMEM((half, n), BF),
            pltpu.SemaphoreType.DMA((nz,)),
        ],
        solve_flops,
        specs=[SMEM, VMEM, VMEM, ANY, VMEM],
    )
    far, _ = after(movers[2:], sent)
    close = [movers[0], swap(movers[1], "loc", nl, 2)]
    far = [swap(x, "loc", nl, 2 * (j + 2)) for j, x in enumerate(far)]

    moved = []
    for part in (close, far):
        blocks = call(
            bind(tail_kernel),
            [S((packed, len(part) * LANES), jnp.int16)] * ni,
            [at, mix_a, mix_b, *part],
            [pltpu.VMEM((packed, w), jnp.int32)],
            pass_flops,
        )
        moved += exchange(blocks, "inc", ni)
    sent = call(bind(collect_kernel), [S((packed, w), BF)] * ni, [at, sent])
    sent = exchange(sent, "inc", ni)

    (new_mass,) = call(
        bind(next_mass_kernel),
        [S((rows, plan.columns), F32)],
        [at, *moved, first, second],
        [pltpu.VMEM((packed, w), jnp.int32)] + [pltpu.VMEM((ni, packed, w), BF)] * 2,
        4 * pass_flops,
    )
    (new_value,) = call(
        bind(value_kernel),
        [S((rows, plan.columns), F32)],
        [at, *sent, hit, second, flow_util],
        [pltpu.VMEM((ni, packed, w), BF)],
        2 * pass_flops,
    )
    return new_value, new_mass


def gathered(cont_value, flow_util, move_cost, live_mask, trans_weight, asset_policy, mass):
    high = lax.Precision.HIGHEST
    e, a = asset_policy.shape
    raised = trans_weight + 16.0 * jnp.eye(e, dtype=F32)
    trans_prob = raised / jnp.sum(raised, axis=1, keepdims=True)
    onehot = (asset_policy[:, :, None] == jnp.arange(a, dtype=jnp.int32)[None, None, :]).astype(F32)
    moved_rows = lax.all_to_all(cont_value, "inc", split_axis=0, concat_axis=1, tiled=True)
    expect = jnp.einsum("ef,jfb->jeb", trans_prob, moved_rows.reshape(-1, e, a), precision=high)
    chosen_all = jnp.einsum("jeb,eab->jea", expect, onehot, precision=high).reshape(-1, e * a)
    chosen = lax.all_to_all(chosen_all, "inc", split_axis=1, concat_axis=0, tiled=True)
    scores = DISCOUNT * chosen
    live_rows = live_mask[:, None] > 0
    local_max = jnp.max(jnp.where(live_rows, scores, F32(-1e30)), axis=0)
    column_max = lax.pmax(local_max, "loc")
    dest_weight = jnp.where(live_rows, jnp.exp(scores - column_max[None, :]), F32(0.0)).astype(BF)
    kernel = jnp.exp(-move_cost).astype(BF)
    totals = dot(kernel, lax.all_gather(dest_weight, "loc", axis=0, tiled=True))
    new_value = flow_util + column_max[None, :] + jnp.log(totals)
    shares = (mass / totals).astype(BF)
    arrived = lax.psum_scatter(
        lax.dot_general(
            kernel, shares, (((0,), (0,)), ((), ())), preferred_element_type=F32
        ).astype(BF),
        "loc",
        scatter_dimension=0,
        tiled=True,
    ).astype(F32)
    movers = dest_weight.astype(F32) * arrived
    moved_mass = lax.all_to_all(movers, "inc", split_axis=0, concat_axis=1, tiled=True)
    shuffled = jnp.einsum("jea,eab->jeb", moved_mass.reshape(-1, e, a), onehot, precision=high)
    mixed_mass = jnp.einsum("ef,jeb->jfb", trans_prob, shuffled, precision=high).reshape(-1, e * a)
    new_mass = lax.all_to_all(mixed_mass, "inc", split_axis=1, concat_axis=0, tiled=True)
    return new_value, new_mass


def solution(mesh):
    n_loc, n_inc = mesh.shape["loc"], mesh.shape["inc"]

    def shards(*args):
        rows, columns = args[0].shape
        plan = Plan(n_loc, n_inc, args[2].shape[1], rows, columns, *args[5].shape)
        if plan.fits():
            return state_split(plan, *args)
        return gathered(*args)

    split = P("loc", "inc")
    return jax.shard_map(
        shards,
        mesh=mesh,
        in_specs=(split, split, P("loc", None), P("loc"), P(), P(), split),
        out_specs=(split, split),
        check_vma=False,
    )
```

```python
import functools
import math

import jax
import jax.numpy as jnp
from jax import lax
from jax.experimental import pallas as pl
from jax.experimental.pallas import tpu as pltpu
from jax.sharding import PartitionSpec as P

DISCOUNT = 0.96
LANES = 128
TILE = 16
VALUE_LOW = -4.0
VALUE_HIGH = 252.0
STEP = (VALUE_HIGH - VALUE_LOW) / 65535.0
HALF = 32768.0
LN2 = math.log(2.0)
SCORE_STEP = DISCOUNT * STEP / LN2
SCORE_SHIFT = DISCOUNT * (HALF * STEP + VALUE_LOW)

BF = jnp.bfloat16
F32 = jnp.float32
VMEM = pl.BlockSpec(memory_space=pltpu.VMEM)
SMEM = pl.BlockSpec(memory_space=pltpu.SMEM)
ANY = pl.BlockSpec(memory_space=pl.ANY)


def dot(a, b):
    return lax.dot_general(a, b, (((1,), (0,)), ((), ())), preferred_element_type=F32)


def dot_nt(a, b):
    return lax.dot_general(a, b, (((1,), (1,)), ((), ())), preferred_element_type=F32)


def lanes_at(start, size):
    return pl.ds(pl.multiple_of(start, LANES), size)


def call(kernel, outs, ins, scratch=(), flops=0, specs=None, out_specs=None, vmem=48):
    moved = sum(math.prod(x.shape) * x.dtype.itemsize for x in list(ins) + list(outs))
    return pl.pallas_call(
        kernel,
        out_shape=tuple(outs),
        in_specs=specs or [SMEM] + [VMEM] * (len(ins) - 1),
        out_specs=tuple(out_specs or [VMEM] * len(outs)),
        scratch_shapes=list(scratch),
        compiler_params=pltpu.CompilerParams(vmem_limit_bytes=vmem * 1024 * 1024),
        cost_estimate=pl.CostEstimate(flops=flops, bytes_accessed=moved, transcendentals=0),
    )(*ins)


class Plan:
    def __init__(self, n_loc, n_inc, counties, rows, columns, incomes, assets):
        self.n_loc, self.n_inc, self.n_z = n_loc, n_inc, n_loc // 2
        self.counties, self.rows, self.columns = counties, rows, columns
        self.incomes, self.assets = incomes, assets
        self.own_incomes = incomes // n_inc
        self.own_assets = assets // n_inc
        self.group_assets = LANES // self.own_incomes
        self.wide = n_inc * LANES
        self.packed = rows + TILE
        self.half = counties // 2
        self.block_rows = counties // LANES
        self.window = (self.block_rows // 2 + 1) * LANES
        self.stride = rows // n_inc // TILE * TILE
        self.quarter = rows - self.stride * (n_inc - 1)
        self.cut = (self.window // LANES + 1) // 2 * LANES

    def fits(self):
        power = lambda n: n > 1 and n & (n - 1) == 0
        return (
            power(self.n_loc)
            and power(self.n_z)
            and power(self.n_inc)
            and self.incomes == LANES
            and self.own_incomes * self.group_assets == LANES
            and self.columns == self.n_z * self.wide
            and self.n_z == self.n_inc == 4
            and self.own_assets == self.n_z * self.group_assets
            and self.rows % TILE == 0
            and self.counties == self.rows * self.n_loc
            and self.counties % LANES == 0
            and self.block_rows % 2 == 1
        )


def order_maps(plan):
    w, oa, oi = plan.wide, plan.own_assets, plan.own_incomes
    r = lax.broadcasted_iota(jnp.int32, (w, w), 0)
    c = lax.broadcasted_iota(jnp.int32, (w, w), 1)
    a = plan.assets
    spot = (r % a) // oa * LANES + r // a * oa + r % oa
    first = (c == spot).astype(BF)
    second = (c == r % oa * oi + r // oa).astype(BF)
    return first, second


def encode_kernel(plan, at, value, first, second, *refs):
    outs, (high, low) = refs[: plan.n_inc], refs[plan.n_inc :]
    inc, w = at[1], plan.wide
    for t in range(plan.n_inc):
        x = value[:, t * w : (t + 1) * w]
        code = jnp.clip(jnp.round((x - VALUE_LOW) * (1.0 / STEP)) - HALF, -HALF, HALF - 1.0)
        top = jnp.floor(code * (1.0 / 256.0))
        rest = code - 256.0 * top
        moved_top = dot(top.astype(BF), first[...]).astype(BF)
        moved_rest = dot(rest.astype(BF), first[...]).astype(BF)
        for q in range(plan.n_inc):
            high[q, :, t * LANES : (t + 1) * LANES] = moved_top[:, q * LANES : (q + 1) * LANES]
            low[q, :, t * LANES : (t + 1) * LANES] = moved_rest[:, q * LANES : (q + 1) * LANES]
    for k in range(plan.n_inc):
        q = inc ^ k
        code = dot(high[q], second[...]) * 256.0 + dot(low[q], second[...])
        outs[k][...] = code.astype(jnp.int32).astype(jnp.int16)


def weight_kernel(plan, at, *refs):
    ni, nz, rows = plan.n_inc, plan.n_z, plan.rows
    codes, (mix_a, mix_b, live), refs = refs[:ni], refs[ni : ni + 3], refs[ni + 3 :]
    weights, held = refs
    inc, w = at[1], plan.wide
    alive = live[...] > 0.0
    for g in range(nz):
        for k in range(ni):
            held[:, lanes_at((inc ^ k) * LANES, LANES)] = codes[k][
                :, g * LANES : (g + 1) * LANES
            ].astype(jnp.int32)
        code = held[...]
        top = (code >> 8).astype(F32).astype(BF)
        rest = (code & 255).astype(F32).astype(BF)
        mixed = (dot(top, mix_a[...]) + dot(top, mix_b[...])) * 256.0 + dot(rest, mix_a[...])
        score = mixed * SCORE_STEP
        peak = jnp.max(jnp.where(alive, score, -512.0), axis=0, keepdims=True)
        peak = jnp.ceil(peak)
        weights[g, 0:rows, :] = jnp.where(alive, jnp.exp2(score - peak), 0.0).astype(BF)
        weights[g, rows:, :] = jnp.broadcast_to(peak, (TILE, w)).astype(BF)


def mass_kernel(plan, at, mass, hit, second, *refs):
    outs, (held,) = refs[: plan.n_inc], refs[plan.n_inc :]
    inc, w = at[1], plan.wide
    for t in range(plan.n_inc):
        x = mass[:, t * w : (t + 1) * w]
        top = x.astype(BF)
        rest = (x - top.astype(F32)).astype(BF)
        moved = (dot(top, hit[t]) + dot(rest, hit[t])).astype(BF)
        for q in range(plan.n_inc):
            held[q, :, t * LANES : (t + 1) * LANES] = moved[:, q * LANES : (q + 1) * LANES]
    for k in range(plan.n_inc):
        outs[k][...] = dot(held[inc ^ k], second[...]).astype(BF)


def spread_kernel(plan, at, *refs):
    *ins, out = refs
    for k in range(plan.n_inc):
        for g in range(plan.n_z):
            out[g, :, lanes_at((at[1] ^ k) * LANES, LANES)] = ins[k][
                :, g * LANES : (g + 1) * LANES
            ]


def collect_kernel(plan, at, *refs):
    blocks, *outs = refs
    for k in range(plan.n_inc):
        for g in range(plan.n_z):
            outs[k][:, g * LANES : (g + 1) * LANES] = blocks[
                g, :, lanes_at((at[1] ^ k) * LANES, LANES)
            ]


def windows(plan, start, count, near, held, out):
    n = plan.counties
    held[:, :n] = near
    held[:, n:] = near[:, : plan.window - LANES]
    for g in range(count // TILE):
        block = (start + g * TILE) // LANES
        out[g * TILE : (g + 1) * TILE, :] = held[
            g * TILE : (g + 1) * TILE, lanes_at(block * LANES, plan.window)
        ]


def quarter_kernel(plan, at, cost, out, part, held, sem):
    start = pl.multiple_of(at[1] * plan.stride, TILE)
    copy = pltpu.make_async_copy(cost.at[pl.ds(start, plan.quarter)], part, sem)
    copy.start()
    copy.wait()
    near = jnp.exp(-part[...]).astype(BF)
    windows(plan, at[0] * plan.rows + start, plan.quarter, near, held, out)


def window_kernel(plan, at, cost, out, held):
    near = jnp.exp(-cost[...]).astype(BF)
    windows(plan, at[0] * plan.rows, plan.rows, near, held, out)


def county_rows(plan, at, z, side):
    start = (2 * z + ((at[0] % 2) ^ side)) * plan.rows
    return pl.ds(pl.multiple_of(start, TILE), plan.rows)


def near_copies(plan, near, held, sems):
    blocks = [pl.ds(j * plan.rows, plan.rows) for j in range(plan.n_z)]
    return [
        pltpu.make_async_copy(near.at[b], held.at[b], sems.at[j]) for j, b in enumerate(blocks)
    ]


def total_kernel(plan, at, *refs):
    nz, rows, cut = plan.n_z, plan.rows, plan.cut
    own_weights, other_weights, refs = refs[0], refs[1], refs[2:]
    both, (sent, scaled, near, weight, strip, full, sums, sem) = refs[:10], refs[10:]
    z, core, inc = at[0] // 2, at[0] % 2, at[1]
    left, right = pl.ds(0, cut), pl.ds(cut, plan.window - cut)
    always, last = [], []
    for side in range(2):
        own, *parts = both[side * 5 : side * 5 + 5]
        first_row = lambda j: (2 * (z ^ j) + (core ^ side)) * rows
        always.append((own, strip.at[pl.ds(pl.multiple_of(first_row(0), TILE), rows)]))
        places = ((0, 1), left), ((2, 3), left), ((0, 2), right), ((1, 3), right)
        for part, (steps, lanes) in zip(parts, places):
            for h, k in enumerate(steps):
                q = inc ^ k
                for j in range(1, nz):
                    base = (h * (nz - 1) + j - 1) * plan.quarter
                    start = first_row(j) + q * plan.stride
                    rest = plan.quarter - plan.stride
                    to = lambda r, size: strip.at[pl.ds(pl.multiple_of(r, TILE), size), lanes]
                    always.append((part.at[pl.ds(base, plan.stride)], to(start, plan.stride)))
                    extra = part.at[pl.ds(base + plan.stride, rest)]
                    last.append((q == plan.n_inc - 1, extra, to(start + plan.stride, rest)))
    copies = [pltpu.make_async_copy(a, b, sem) for a, b in always]
    more = [(c, pltpu.make_async_copy(a, b, sem)) for c, a, b in last]
    for c in copies:
        c.start()
    for when, c in more:
        pl.when(when)(c.start)

    places = [(x, g) for x in (own_weights, other_weights) for g in range(nz)]
    peaks = [x[g, rows : rows + 1, :].astype(F32) for x, g in places]
    peak = functools.reduce(jnp.maximum, peaks)
    for i, (x, g) in enumerate(places):
        part = (x[g, :rows, :].astype(F32) * jnp.exp2(peaks[i] - peak)).astype(BF)
        weight[county_rows(plan, at, g, i // nz), :] = part
        if i < nz:
            scaled[g] = part

    for c in copies:
        c.wait()
    for when, c in more:
        pl.when(when)(c.wait)
    blocks = plan.block_rows
    for i in range(blocks):
        for k in range(plan.window // LANES):
            j = (i + k) % blocks
            tile = strip[i * LANES : (i + 1) * LANES, k * LANES : (k + 1) * LANES]
            full[i * LANES : (i + 1) * LANES, j * LANES : (j + 1) * LANES] = tile
            if k:
                full[j * LANES : (j + 1) * LANES, i * LANES : (i + 1) * LANES] = tile.T
    copies = []
    for j in range(nz):
        out = near.at[pl.ds(j * rows, rows)]
        copies.append(pltpu.make_async_copy(full.at[county_rows(plan, at, j, 0)], out, sem))
    for c in copies:
        c.start()
    def product(j, carry):
        sums[j] = dot(full[county_rows(plan, at, j, 0), :], weight[...])
        return carry

    lax.fori_loop(0, nz, product, 0)
    sent[:, :rows, :] = sums[...].astype(BF)
    sent[:, rows:, :] = jnp.broadcast_to(peak[None], (nz, TILE, plan.wide)).astype(BF)
    for c in copies:
        c.wait()


def share_kernel(plan, masses, totals, out):
    for g in range(plan.n_z):
        total = totals[g, : plan.rows, :].astype(F32)
        out[g] = (masses[g].astype(F32) / total).astype(BF)


def mover_kernel(plan, at, own, other, near, scaled, *refs):
    nz, rows = plan.n_z, plan.rows
    outs, (movers, share, held, sems) = refs[:nz], refs[nz:]
    copies = near_copies(plan, near, held, sems)
    for c in copies:
        c.start()
    for side, x in enumerate((own, other)):
        for g in range(nz):
            share[county_rows(plan, at, g, side), :] = x[g]
    for g in range(nz):
        copies[g].wait()
        arrived = dot(held[g * rows : (g + 1) * rows, :], share[...])
        movers[g] = (scaled[g].astype(F32) * arrived).astype(BF)
    for j in range(nz):
        outs[j][...] = movers[(at[0] // 2) ^ j]


def code_blocks(plan, mix_a, mix_b, ins, mixed):
    rows = plan.rows
    for i, part in enumerate(ins):
        x = part[...]
        new = dot_nt(x, mix_a[...]) + dot_nt(x, mix_b[...])
        most = jnp.maximum(jnp.max(new, axis=0, keepdims=True), 1e-30)
        power = jnp.ceil(jnp.log2(most))
        code = jnp.minimum(jnp.round(new * jnp.exp2(15.0 - power)), HALF - 1.0)
        mixed[:rows, :] = code.astype(jnp.int32)
        mixed[rows:, :] = jnp.broadcast_to(power, (TILE, plan.wide)).astype(jnp.int32)
        yield i


def tail_kernel(plan, at, mix_a, mix_b, *refs):
    ins, outs, mixed = refs[: -1 - plan.n_inc], refs[-1 - plan.n_inc : -1], refs[-1]
    for i in code_blocks(plan, mix_a, mix_b, ins, mixed):
        for k in range(plan.n_inc):
            block = mixed[:, lanes_at((at[1] ^ k) * LANES, LANES)].astype(jnp.int16)
            outs[k][:, i * LANES : (i + 1) * LANES] = block


def next_mass_kernel(plan, at, *refs):
    ni, w, rows = plan.n_inc, plan.wide, plan.rows
    close, far, refs = refs[:ni], refs[ni : 2 * ni], refs[2 * ni :]
    first, second, out, held, high, low = refs
    z, inc = at[0] // 2, at[1]
    for k in range(ni):
        j = 0
        for part in (close[k], far[k]):
            for i in range(part.shape[1] // LANES):
                held[:, lanes_at((z ^ j) * LANES, LANES)] = part[
                    :, i * LANES : (i + 1) * LANES
                ].astype(jnp.int32)
                j += 1
        code = held[...]
        for part, into in ((code >> 8, high), (code & 255, low)):
            back = dot_nt(part.astype(F32).astype(BF), second[...]).astype(BF)
            for t in range(ni):
                into[t, :, lanes_at((inc ^ k) * LANES, LANES)] = back[:, t * LANES : (t + 1) * LANES]
    for t in range(ni):
        code = dot_nt(high[t], first[...]) * 256.0 + dot_nt(low[t], first[...])
        out[:, t * w : (t + 1) * w] = code[:rows, :] * jnp.exp2(code[rows : rows + 1, :] - 15.0)


def value_kernel(plan, at, *refs):
    ni, w, rows = plan.n_inc, plan.wide, plan.rows
    ins, (hit, second, flow), (out, held) = refs[:ni], refs[ni : ni + 3], refs[ni + 3 :]
    inc = at[1]
    for k in range(ni):
        back = dot_nt(ins[k][...], second[...]).astype(BF)
        for t in range(ni):
            held[t, :, lanes_at((inc ^ k) * LANES, LANES)] = back[:, t * LANES : (t + 1) * LANES]
    for t in range(ni):
        got = dot_nt(held[t], hit[t])
        peak = got[rows : rows + 1, :] * LN2 + SCORE_SHIFT
        out[:, t * w : (t + 1) * w] = flow[:, t * w : (t + 1) * w] + (peak + jnp.log(got[:rows, :]))


def mix_kernel(plan, trans, out_a, out_b):
    e, oi, ga, w = plan.incomes, plan.own_incomes, plan.group_assets, plan.wide
    grid = lambda shape, axis: lax.broadcasted_iota(jnp.int32, shape, axis)
    raised = trans[...] + jnp.where(grid((e, e), 0) == grid((e, e), 1), 16.0, 0.0)
    prob = (raised / jnp.sum(raised, axis=1, keepdims=True)).T
    lane = grid((e, w), 1)
    place = (grid((e, w), 0) == lane // LANES * oi + lane % oi).astype(BF)
    same = grid((w, w), 0) // oi % ga == grid((w, w), 1) // oi % ga
    top = prob.astype(BF)
    for part, out in ((top, out_a), ((prob - top.astype(F32)).astype(BF), out_b)):
        wide = dot(part, place)
        blocks = [wide[i * oi : (i + 1) * oi] for i in range(plan.n_inc) for _ in range(ga)]
        out[...] = jnp.where(same, jnp.concatenate(blocks, axis=0), 0.0).astype(BF)


def policy_maps(plan, asset_policy, inc):
    ni, oa, a, w = plan.n_inc, plan.own_assets, plan.assets, plan.wide
    own = lax.dynamic_slice_in_dim(asset_policy, inc * plan.own_incomes, plan.own_incomes, 0)
    group = w // a
    row_income = jnp.arange(group, dtype=jnp.int32)[None, :, None]
    own = own.reshape(ni, group, a)
    lane = own // oa * LANES + row_income * oa + own % oa
    lane = lane.reshape(ni, w, 1)
    return (lane == lax.broadcasted_iota(jnp.int32, (ni, w, w), 2)).astype(BF)


def swap(x, axis, n, k):
    return lax.ppermute(x, axis, [(s, s ^ k) for s in range(n)]) if k else x


def exchange(blocks, axis, n, unit=1):
    got = {k: swap(blocks[k], axis, n, k * unit) for k in reversed(range(len(blocks)))}
    return [got[k] for k in range(len(blocks))]


def after(x, y):
    return lax.optimization_barrier((x, y))


def state_split(plan, cont_value, flow_util, move_cost, live_mask, trans_weight, asset_policy, mass):
    ni, nl, nz, rows, n = plan.n_inc, plan.n_loc, plan.n_z, plan.rows, plan.counties
    w, packed, half = plan.wide, plan.packed, plan.half
    S = jax.ShapeDtypeStruct
    loc, inc = lax.axis_index("loc"), lax.axis_index("inc")
    at = jnp.stack([loc, inc]).astype(jnp.int32)
    bind = lambda f: functools.partial(f, plan)
    pass_flops = 2 * rows * plan.columns * w
    solve_flops = 2 * half * n * w
    swap_core = lambda x: swap(x, "loc", nl, 1)
    lines = [list(range(core, nl, 2)) for core in range(2)]
    along_z = lambda x: lax.all_to_all(x, "loc", 0, 0, axis_index_groups=lines)
    ring = n + plan.window - LANES

    (quarter,) = call(
        bind(quarter_kernel),
        [S((plan.quarter, plan.window), BF)],
        [at, move_cost],
        [
            pltpu.VMEM((plan.quarter, n), F32),
            pltpu.VMEM((plan.quarter, ring), BF),
            pltpu.SemaphoreType.DMA,
        ],
        specs=[SMEM, ANY],
    )
    pieces = [swap(quarter, "loc", nl, 2 * j) for j in range(2, nz)]

    first, second = order_maps(plan)
    codes = call(
        bind(encode_kernel),
        [S((rows, w), jnp.int16)] * ni,
        [at, cont_value, first, second],
        [pltpu.VMEM((ni, rows, w), BF)] * 2,
        4 * pass_flops,
    )
    codes = exchange(codes, "inc", ni)
    quarter, _ = after(quarter, codes[1])
    pieces.insert(0, swap(quarter, "loc", nl, 2))

    hit = policy_maps(plan, asset_policy, inc)
    masses = call(
        bind(mass_kernel),
        [S((rows, w), BF)] * ni,
        [at, mass, hit, second],
        [pltpu.VMEM((ni, rows, w), BF)],
        3 * pass_flops,
    )
    mix_a, mix_b = call(
        bind(mix_kernel), [S((w, w), BF)] * 2, [trans_weight], specs=[VMEM]
    )
    masses, codes = after(masses, codes)
    masses = exchange(masses, "inc", ni)

    live = (live_mask > 0).astype(F32)[:, None]
    weights = call(
        bind(weight_kernel),
        [S((nz, packed, w), BF)],
        [at, *codes, mix_a, mix_b, live],
        [pltpu.VMEM((rows, w), jnp.int32)],
        3 * pass_flops,
    )
    weights, _ = after(weights[0], pieces)
    weights = along_z(weights)
    others = swap_core(weights)

    strip, _ = after(jnp.concatenate(pieces), masses)
    left, right = strip[:, : plan.cut], strip[:, plan.cut :]
    left = jnp.concatenate([left, swap(left, "inc", ni, 1)])
    right = jnp.concatenate([right, swap(right, "inc", ni, 2)])
    later_cost, _ = after(move_cost, (left, right))
    (own_near,) = call(
        bind(window_kernel),
        [S((rows, plan.window), BF)],
        [at, later_cost],
        [pltpu.VMEM((rows, ring), BF)],
    )
    near = [own_near, left, swap(left, "inc", ni, 2), right, swap(right, "inc", ni, 1)]
    near = near + [swap_core(x) for x in near]

    masses = call(bind(spread_kernel), [S((nz, rows, w), BF)], [at, *masses])
    masses, weights = after(masses[0], weights)
    masses = along_z(masses)

    totals, scaled, near = call(
        bind(total_kernel),
        [S((nz, packed, w), BF), S((nz, rows, w), BF), S((half, n), BF)],
        [at, weights, others, *near],
        [
            pltpu.VMEM((n, w), BF),
            pltpu.VMEM((n, plan.window), BF),
            pltpu.VMEM((n, n), BF),
            pltpu.VMEM((nz, rows, w), F32),
            pltpu.SemaphoreType.DMA,
        ],
        solve_flops,
        specs=[SMEM, VMEM, VMEM] + [ANY] * len(near),
        out_specs=[VMEM, VMEM, ANY],
        vmem=60,
    )
    sent = along_z(totals)
    (share,) = call(
        bind(share_kernel), [S((nz, rows, w), BF)], [masses, totals], specs=[VMEM] * 2
    )
    movers = call(
        bind(mover_kernel),
        [S((rows, w), BF)] * nz,
        [at, share, swap_core(share), near, scaled],
        [
            pltpu.VMEM((nz, rows, w), BF),
            pltpu.VMEM((n, w), BF),
            pltpu.VMEM((half, n), BF),
            pltpu.SemaphoreType.DMA((nz,)),
        ],
        solve_flops,
        specs=[SMEM, VMEM, VMEM, ANY, VMEM],
    )
    far, _ = after(movers[2:], sent)
    close = [movers[0], swap(movers[1], "loc", nl, 2)]
    far = [swap(x, "loc", nl, 2 * (j + 2)) for j, x in enumerate(far)]

    pack = lambda part, outs, kernel: call(
        bind(kernel),
        outs,
        [at, mix_a, mix_b, *part],
        [pltpu.VMEM((packed, w), jnp.int32)],
        pass_flops,
    )
    close = pack(close, [S((packed, 2 * LANES), jnp.int16)] * ni, tail_kernel)
    close = exchange(close, "inc", ni)
    sent = call(bind(collect_kernel), [S((packed, w), BF)] * ni, [at, sent])
    sent = exchange(sent, "inc", ni)
    (new_value,) = call(
        bind(value_kernel),
        [S((rows, plan.columns), F32)],
        [at, *sent, hit, second, flow_util],
        [pltpu.VMEM((ni, packed, w), BF)],
        2 * pass_flops,
    )
    far, _ = after(far, (close, new_value))
    far = pack(far, [S((packed, 2 * LANES), jnp.int16)] * ni, tail_kernel)
    far = exchange(far, "inc", ni)
    (new_mass,) = call(
        bind(next_mass_kernel),
        [S((rows, plan.columns), F32)],
        [at, *close, *far, first, second],
        [pltpu.VMEM((packed, w), jnp.int32)] + [pltpu.VMEM((ni, packed, w), BF)] * 2,
        4 * pass_flops,
    )
    return new_value, new_mass


def gathered(cont_value, flow_util, move_cost, live_mask, trans_weight, asset_policy, mass):
    high = lax.Precision.HIGHEST
    e, a = asset_policy.shape
    raised = trans_weight + 16.0 * jnp.eye(e, dtype=F32)
    trans_prob = raised / jnp.sum(raised, axis=1, keepdims=True)
    onehot = (asset_policy[:, :, None] == jnp.arange(a, dtype=jnp.int32)[None, None, :]).astype(F32)
    moved_rows = lax.all_to_all(cont_value, "inc", split_axis=0, concat_axis=1, tiled=True)
    expect = jnp.einsum("ef,jfb->jeb", trans_prob, moved_rows.reshape(-1, e, a), precision=high)
    chosen_all = jnp.einsum("jeb,eab->jea", expect, onehot, precision=high).reshape(-1, e * a)
    chosen = lax.all_to_all(chosen_all, "inc", split_axis=1, concat_axis=0, tiled=True)
    scores = DISCOUNT * chosen
    live_rows = live_mask[:, None] > 0
    local_max = jnp.max(jnp.where(live_rows, scores, F32(-1e30)), axis=0)
    column_max = lax.pmax(local_max, "loc")
    dest_weight = jnp.where(live_rows, jnp.exp(scores - column_max[None, :]), F32(0.0)).astype(BF)
    kernel = jnp.exp(-move_cost).astype(BF)
    totals = dot(kernel, lax.all_gather(dest_weight, "loc", axis=0, tiled=True))
    new_value = flow_util + column_max[None, :] + jnp.log(totals)
    shares = (mass / totals).astype(BF)
    arrived = lax.psum_scatter(
        lax.dot_general(
            kernel, shares, (((0,), (0,)), ((), ())), preferred_element_type=F32
        ).astype(BF),
        "loc",
        scatter_dimension=0,
        tiled=True,
    ).astype(F32)
    movers = dest_weight.astype(F32) * arrived
    moved_mass = lax.all_to_all(movers, "inc", split_axis=0, concat_axis=1, tiled=True)
    shuffled = jnp.einsum("jea,eab->jeb", moved_mass.reshape(-1, e, a), onehot, precision=high)
    mixed_mass = jnp.einsum("ef,jeb->jfb", trans_prob, shuffled, precision=high).reshape(-1, e * a)
    new_mass = lax.all_to_all(mixed_mass, "inc", split_axis=1, concat_axis=0, tiled=True)
    return new_value, new_mass


def solution(mesh):
    n_loc, n_inc = mesh.shape["loc"], mesh.shape["inc"]

    def shards(*args):
        rows, columns = args[0].shape
        plan = Plan(n_loc, n_inc, args[2].shape[1], rows, columns, *args[5].shape)
        if plan.fits():
            return state_split(plan, *args)
        return gathered(*args)

    split = P("loc", "inc")
    return jax.shard_map(
        shards,
        mesh=mesh,
        in_specs=(split, split, P("loc", None), P("loc"), P(), P(), split),
        out_specs=(split, split),
        check_vma=False,
    )
```

```python
import functools
import math

import jax
import jax.numpy as jnp
from jax import lax
from jax.experimental import pallas as pl
from jax.experimental.pallas import tpu as pltpu
from jax.sharding import PartitionSpec as P

DISCOUNT = 0.96
LANES = 128
TILE = 16
VALUE_LOW = -4.0
VALUE_HIGH = 252.0
STEP = (VALUE_HIGH - VALUE_LOW) / 65535.0
HALF = 32768.0
LN2 = math.log(2.0)
SCORE_STEP = DISCOUNT * STEP / LN2
SCORE_SHIFT = DISCOUNT * (HALF * STEP + VALUE_LOW)

BF = jnp.bfloat16
F32 = jnp.float32
VMEM = pl.BlockSpec(memory_space=pltpu.VMEM)
SMEM = pl.BlockSpec(memory_space=pltpu.SMEM)
ANY = pl.BlockSpec(memory_space=pl.ANY)


def dot(a, b):
    return lax.dot_general(a, b, (((1,), (0,)), ((), ())), preferred_element_type=F32)


def dot_nt(a, b):
    return lax.dot_general(a, b, (((1,), (1,)), ((), ())), preferred_element_type=F32)


def lanes_at(start, size):
    return pl.ds(pl.multiple_of(start, LANES), size)


def call(kernel, outs, ins, scratch=(), flops=0, specs=None, out_specs=None, vmem=24):
    moved = sum(math.prod(x.shape) * x.dtype.itemsize for x in list(ins) + list(outs))
    return pl.pallas_call(
        kernel,
        out_shape=tuple(outs),
        in_specs=specs or [SMEM] + [VMEM] * (len(ins) - 1),
        out_specs=tuple(out_specs or [VMEM] * len(outs)),
        scratch_shapes=list(scratch),
        compiler_params=pltpu.CompilerParams(vmem_limit_bytes=vmem * 1024 * 1024),
        cost_estimate=pl.CostEstimate(flops=flops, bytes_accessed=moved, transcendentals=0),
    )(*ins)


class Plan:
    def __init__(self, n_loc, n_inc, counties, rows, columns, incomes, assets):
        self.n_loc, self.n_inc, self.n_z = n_loc, n_inc, n_loc // 2
        self.counties, self.rows, self.columns = counties, rows, columns
        self.incomes, self.assets = incomes, assets
        self.own_incomes = incomes // n_inc
        self.own_assets = assets // n_inc
        self.group_assets = LANES // self.own_incomes
        self.wide = n_inc * LANES
        self.packed = rows + TILE
        self.half = counties // 2
        self.block_rows = counties // LANES
        self.window = (self.block_rows // 2 + 1) * LANES
        self.stride = rows // n_inc // TILE * TILE
        self.quarter = rows - self.stride * (n_inc - 1)
        self.cut = (self.window // LANES + 1) // 2 * LANES

    def fits(self):
        power = lambda n: n > 1 and n & (n - 1) == 0
        return (
            power(self.n_loc)
            and power(self.n_z)
            and power(self.n_inc)
            and self.incomes == LANES
            and self.own_incomes * self.group_assets == LANES
            and self.columns == self.n_z * self.wide
            and self.n_z == self.n_inc == 4
            and self.own_assets == self.n_z * self.group_assets
            and self.rows % TILE == 0
            and self.counties == self.rows * self.n_loc
            and self.counties % LANES == 0
            and self.block_rows % 2 == 1
        )


def order_maps(plan):
    w, oa, oi = plan.wide, plan.own_assets, plan.own_incomes
    r = lax.broadcasted_iota(jnp.int32, (w, w), 0)
    c = lax.broadcasted_iota(jnp.int32, (w, w), 1)
    a = plan.assets
    spot = (r % a) // oa * LANES + r // a * oa + r % oa
    first = (c == spot).astype(BF)
    second = (c == r % oa * oi + r // oa).astype(BF)
    return first, second


def encode_kernel(plan, at, value, first, second, *refs):
    outs, (high, low) = refs[: plan.n_inc], refs[plan.n_inc :]
    inc, w = at[1], plan.wide
    for t in range(plan.n_inc):
        x = value[:, t * w : (t + 1) * w]
        code = jnp.clip(jnp.round((x - VALUE_LOW) * (1.0 / STEP)) - HALF, -HALF, HALF - 1.0)
        top = jnp.floor(code * (1.0 / 256.0))
        rest = code - 256.0 * top
        moved_top = dot(top.astype(BF), first[...]).astype(BF)
        moved_rest = dot(rest.astype(BF), first[...]).astype(BF)
        for q in range(plan.n_inc):
            high[q, :, t * LANES : (t + 1) * LANES] = moved_top[:, q * LANES : (q + 1) * LANES]
            low[q, :, t * LANES : (t + 1) * LANES] = moved_rest[:, q * LANES : (q + 1) * LANES]
    for k in range(plan.n_inc):
        q = inc ^ k
        code = dot(high[q], second[...]) * 256.0 + dot(low[q], second[...])
        outs[k][...] = code.astype(jnp.int32).astype(jnp.int16)


def weight_kernel(plan, at, *refs):
    ni, nz, rows = plan.n_inc, plan.n_z, plan.rows
    codes, (mix_a, mix_b, live), refs = refs[:ni], refs[ni : ni + 3], refs[ni + 3 :]
    weights, held = refs
    inc, w = at[1], plan.wide
    alive = live[...] > 0.0
    for g in range(nz):
        for k in range(ni):
            held[:, lanes_at((inc ^ k) * LANES, LANES)] = codes[k][
                :, g * LANES : (g + 1) * LANES
            ].astype(jnp.int32)
        code = held[...]
        top = (code >> 8).astype(F32).astype(BF)
        rest = (code & 255).astype(F32).astype(BF)
        mixed = (dot(top, mix_a[...]) + dot(top, mix_b[...])) * 256.0 + dot(rest, mix_a[...])
        score = mixed * SCORE_STEP
        peak = jnp.max(jnp.where(alive, score, -512.0), axis=0, keepdims=True)
        peak = jnp.ceil(peak)
        weights[g, 0:rows, :] = jnp.where(alive, jnp.exp2(score - peak), 0.0).astype(BF)
        weights[g, rows:, :] = jnp.broadcast_to(peak, (TILE, w)).astype(BF)


def mass_kernel(plan, at, mass, hit, second, *refs):
    outs, (held,) = refs[: plan.n_inc], refs[plan.n_inc :]
    inc, w = at[1], plan.wide
    for t in range(plan.n_inc):
        x = mass[:, t * w : (t + 1) * w]
        top = x.astype(BF)
        rest = (x - top.astype(F32)).astype(BF)
        moved = (dot(top, hit[t]) + dot(rest, hit[t])).astype(BF)
        for q in range(plan.n_inc):
            held[q, :, t * LANES : (t + 1) * LANES] = moved[:, q * LANES : (q + 1) * LANES]
    for k in range(plan.n_inc):
        outs[k][...] = dot(held[inc ^ k], second[...]).astype(BF)


def spread_kernel(plan, at, *refs):
    *ins, out = refs
    for k in range(plan.n_inc):
        for g in range(plan.n_z):
            out[g, :, lanes_at((at[1] ^ k) * LANES, LANES)] = ins[k][
                :, g * LANES : (g + 1) * LANES
            ]


def collect_kernel(plan, at, *refs):
    blocks, *outs = refs
    for k in range(plan.n_inc):
        for g in range(plan.n_z):
            outs[k][:, g * LANES : (g + 1) * LANES] = blocks[
                g, :, lanes_at((at[1] ^ k) * LANES, LANES)
            ]


def windows(plan, start, count, near, held, out):
    n = plan.counties
    held[:, :n] = near
    held[:, n:] = near[:, : plan.window - LANES]
    for g in range(count // TILE):
        block = (start + g * TILE) // LANES
        out[g * TILE : (g + 1) * TILE, :] = held[
            g * TILE : (g + 1) * TILE, lanes_at(block * LANES, plan.window)
        ]


def quarter_kernel(plan, at, cost, out, part, held, sem):
    start = pl.multiple_of(at[1] * plan.stride, TILE)
    copy = pltpu.make_async_copy(cost.at[pl.ds(start, plan.quarter)], part, sem)
    copy.start()
    copy.wait()
    near = jnp.exp(-part[...]).astype(BF)
    windows(plan, at[0] * plan.rows + start, plan.quarter, near, held, out)


def window_kernel(plan, at, cost, out, held):
    near = jnp.exp(-cost[...]).astype(BF)
    windows(plan, at[0] * plan.rows, plan.rows, near, held, out)


def county_rows(plan, at, z, side):
    start = (2 * z + ((at[0] % 2) ^ side)) * plan.rows
    return pl.ds(pl.multiple_of(start, TILE), plan.rows)


def near_copies(plan, near, held, sems):
    blocks = [pl.ds(j * plan.rows, plan.rows) for j in range(plan.n_z)]
    return [
        pltpu.make_async_copy(near.at[b], held.at[b], sems.at[j]) for j, b in enumerate(blocks)
    ]


def total_kernel(plan, at, *refs):
    nz, rows, cut = plan.n_z, plan.rows, plan.cut
    own_weights, other_weights, refs = refs[0], refs[1], refs[2:]
    both, (sent, scaled, near, given, weight, strip, full, sums, sems) = refs[:10], refs[10:]
    z, core, inc = at[0] // 2, at[0] % 2, at[1]
    left, right = pl.ds(0, cut), pl.ds(cut, plan.window - cut)
    always = []
    for side in range(2):
        own, *parts = both[side * 5 : side * 5 + 5]
        first_row = lambda j: (2 * (z ^ j) + (core ^ side)) * rows
        here = pl.ds(pl.multiple_of(first_row(0), TILE), rows)
        for half, lanes in enumerate((left, right)):
            always.append((half, None, own.at[:, lanes], strip.at[here, lanes]))
        places = ((0, 1), left), ((2, 3), left), ((0, 2), right), ((1, 3), right)
        for part, (steps, lanes) in zip(parts, places):
            for h, k in enumerate(steps):
                q = inc ^ k
                for j in range(1, nz):
                    base = (h * (nz - 1) + j - 1) * plan.quarter
                    start = first_row(j) + q * plan.stride
                    rest = plan.quarter - plan.stride
                    to = lambda r, size: strip.at[pl.ds(pl.multiple_of(r, TILE), size), lanes]
                    half = int(lanes is right)
                    always.append((half, None, part.at[pl.ds(base, plan.stride)], to(start, plan.stride)))
                    extra, when = part.at[pl.ds(base + plan.stride, rest)], q == plan.n_inc - 1
                    always.append((half, when, extra, to(start + plan.stride, rest)))
    loads = [pltpu.make_async_copy(own_weights, given.at[0], sems.at[0])]
    loads.append(pltpu.make_async_copy(other_weights, given.at[1], sems.at[0]))
    for c in loads:
        c.start()
    copies = [[], []]
    for half, when, a, b in always:
        copies[half].append((when, pltpu.make_async_copy(a, b, sems.at[1 + half])))
    for when, c in copies[0] + copies[1]:
        pl.when(when)(c.start) if when is not None else c.start()

    for c in loads:
        c.wait()
    places = [(side, g) for side in range(2) for g in range(nz)]
    peaks = [given[side, g, rows : rows + 1, :].astype(F32) for side, g in places]
    peak = functools.reduce(jnp.maximum, peaks)
    for (side, g), own_peak in zip(places, peaks):
        part = (given[side, g, :rows, :].astype(F32) * jnp.exp2(own_peak - peak)).astype(BF)
        weight[county_rows(plan, at, g, side), :] = part
        if side == 0:
            scaled[g] = part

    blocks, cuts = plan.block_rows, (0, cut // LANES, plan.window // LANES)
    for half in range(2):
        for when, c in copies[half]:
            pl.when(when)(c.wait) if when is not None else c.wait()
        for i in range(blocks):
            for k in range(cuts[half], cuts[half + 1]):
                j = (i + k) % blocks
                tile = strip[i * LANES : (i + 1) * LANES, k * LANES : (k + 1) * LANES]
                full[i * LANES : (i + 1) * LANES, j * LANES : (j + 1) * LANES] = tile
                if k:
                    full[j * LANES : (j + 1) * LANES, i * LANES : (i + 1) * LANES] = tile.T
    copies = []
    for j in range(nz):
        out = near.at[pl.ds(j * rows, rows)]
        copies.append(
            pltpu.make_async_copy(full.at[county_rows(plan, at, j, 0)], out, sems.at[0])
        )
    for c in copies:
        c.start()
    def product(j, carry):
        sums[j] = dot(full[county_rows(plan, at, j, 0), :], weight[...])
        return carry

    lax.fori_loop(0, nz, product, 0)
    sent[:, :rows, :] = sums[...].astype(BF)
    sent[:, rows:, :] = jnp.broadcast_to(peak[None], (nz, TILE, plan.wide)).astype(BF)
    for c in copies:
        c.wait()


def share_kernel(plan, masses, totals, out):
    for g in range(plan.n_z):
        total = totals[g, : plan.rows, :].astype(F32)
        out[g] = (masses[g].astype(F32) / total).astype(BF)


def mover_kernel(plan, at, own, other, near, scaled, *refs):
    nz, rows = plan.n_z, plan.rows
    outs, (movers, share, held, sems) = refs[:nz], refs[nz:]
    copies = near_copies(plan, near, held, sems)
    for c in copies:
        c.start()
    for side, x in enumerate((own, other)):
        for g in range(nz):
            share[county_rows(plan, at, g, side), :] = x[g]
    for g in range(nz):
        copies[g].wait()
        arrived = dot(held[g * rows : (g + 1) * rows, :], share[...])
        movers[g] = (scaled[g].astype(F32) * arrived).astype(BF)
    for j in range(nz):
        outs[j][...] = movers[(at[0] // 2) ^ j]


def code_blocks(plan, mix_a, mix_b, ins, mixed):
    rows = plan.rows
    for i, part in enumerate(ins):
        x = part[...]
        new = dot_nt(x, mix_a[...]) + dot_nt(x, mix_b[...])
        most = jnp.maximum(jnp.max(new, axis=0, keepdims=True), 1e-30)
        power = jnp.ceil(jnp.log2(most))
        code = jnp.minimum(jnp.round(new * jnp.exp2(15.0 - power)), HALF - 1.0)
        mixed[:rows, :] = code.astype(jnp.int32)
        mixed[rows:, :] = jnp.broadcast_to(power, (TILE, plan.wide)).astype(jnp.int32)
        yield i


def tail_kernel(plan, at, mix_a, mix_b, *refs):
    ins, outs, mixed = refs[: -1 - plan.n_inc], refs[-1 - plan.n_inc : -1], refs[-1]
    for i in code_blocks(plan, mix_a, mix_b, ins, mixed):
        for k in range(plan.n_inc):
            block = mixed[:, lanes_at((at[1] ^ k) * LANES, LANES)].astype(jnp.int16)
            outs[k][:, i * LANES : (i + 1) * LANES] = block


def next_mass_kernel(plan, at, *refs):
    ni, w, rows = plan.n_inc, plan.wide, plan.rows
    ins, (first, second, out, held, high, low) = refs[:-6], refs[-6:]
    z, inc = at[0] // 2, at[1]
    for k in range(ni):
        j = 0
        for part in ins[k::ni]:
            for i in range(part.shape[1] // LANES):
                held[:, lanes_at((z ^ j) * LANES, LANES)] = part[
                    :, i * LANES : (i + 1) * LANES
                ].astype(jnp.int32)
                j += 1
        code = held[...]
        for part, into in ((code >> 8, high), (code & 255, low)):
            back = dot_nt(part.astype(F32).astype(BF), second[...]).astype(BF)
            for t in range(ni):
                into[t, :, lanes_at((inc ^ k) * LANES, LANES)] = back[:, t * LANES : (t + 1) * LANES]
    for t in range(ni):
        code = dot_nt(high[t], first[...]) * 256.0 + dot_nt(low[t], first[...])
        out[:, t * w : (t + 1) * w] = code[:rows, :] * jnp.exp2(code[rows : rows + 1, :] - 15.0)


def value_kernel(plan, at, *refs):
    ni, w, rows = plan.n_inc, plan.wide, plan.rows
    ins, (hit, second, flow), (out, held) = refs[:ni], refs[ni : ni + 3], refs[ni + 3 :]
    inc = at[1]
    for k in range(ni):
        back = dot_nt(ins[k][...], second[...]).astype(BF)
        for t in range(ni):
            held[t, :, lanes_at((inc ^ k) * LANES, LANES)] = back[:, t * LANES : (t + 1) * LANES]
    for t in range(ni):
        got = dot_nt(held[t], hit[t])
        peak = got[rows : rows + 1, :] * LN2 + SCORE_SHIFT
        out[:, t * w : (t + 1) * w] = flow[:, t * w : (t + 1) * w] + (peak + jnp.log(got[:rows, :]))


def mix_kernel(plan, trans, out_a, out_b):
    e, oi, ga, w = plan.incomes, plan.own_incomes, plan.group_assets, plan.wide
    grid = lambda shape, axis: lax.broadcasted_iota(jnp.int32, shape, axis)
    raised = trans[...] + jnp.where(grid((e, e), 0) == grid((e, e), 1), 16.0, 0.0)
    prob = (raised / jnp.sum(raised, axis=1, keepdims=True)).T
    lane = grid((e, w), 1)
    place = (grid((e, w), 0) == lane // LANES * oi + lane % oi).astype(BF)
    same = grid((w, w), 0) // oi % ga == grid((w, w), 1) // oi % ga
    top = prob.astype(BF)
    for part, out in ((top, out_a), ((prob - top.astype(F32)).astype(BF), out_b)):
        wide = dot(part, place)
        blocks = [wide[i * oi : (i + 1) * oi] for i in range(plan.n_inc) for _ in range(ga)]
        out[...] = jnp.where(same, jnp.concatenate(blocks, axis=0), 0.0).astype(BF)


def policy_maps(plan, asset_policy, inc):
    ni, oa, a, w = plan.n_inc, plan.own_assets, plan.assets, plan.wide
    own = lax.dynamic_slice_in_dim(asset_policy, inc * plan.own_incomes, plan.own_incomes, 0)
    group = w // a
    row_income = jnp.arange(group, dtype=jnp.int32)[None, :, None]
    own = own.reshape(ni, group, a)
    lane = own // oa * LANES + row_income * oa + own % oa
    lane = lane.reshape(ni, w, 1)
    return (lane == lax.broadcasted_iota(jnp.int32, (ni, w, w), 2)).astype(BF)


def swap(x, axis, n, k):
    return lax.ppermute(x, axis, [(s, s ^ k) for s in range(n)]) if k else x


def exchange(blocks, axis, n, unit=1):
    got = {k: swap(blocks[k], axis, n, k * unit) for k in reversed(range(len(blocks)))}
    return [got[k] for k in range(len(blocks))]


def after(x, y):
    return lax.optimization_barrier((x, y))


def state_split(plan, cont_value, flow_util, move_cost, live_mask, trans_weight, asset_policy, mass):
    ni, nl, nz, rows, n = plan.n_inc, plan.n_loc, plan.n_z, plan.rows, plan.counties
    w, packed, half = plan.wide, plan.packed, plan.half
    S = jax.ShapeDtypeStruct
    loc, inc = lax.axis_index("loc"), lax.axis_index("inc")
    at = jnp.stack([loc, inc]).astype(jnp.int32)
    bind = lambda f: functools.partial(f, plan)
    pass_flops = 2 * rows * plan.columns * w
    solve_flops = 2 * half * n * w
    swap_core = lambda x: swap(x, "loc", nl, 1)
    lines = [list(range(core, nl, 2)) for core in range(2)]
    along_z = lambda x: lax.all_to_all(x, "loc", 0, 0, axis_index_groups=lines)
    ring = n + plan.window - LANES

    (quarter,) = call(
        bind(quarter_kernel),
        [S((plan.quarter, plan.window), BF)],
        [at, move_cost],
        [
            pltpu.VMEM((plan.quarter, n), F32),
            pltpu.VMEM((plan.quarter, ring), BF),
            pltpu.SemaphoreType.DMA,
        ],
        specs=[SMEM, ANY],
    )
    pieces = [swap(quarter, "loc", nl, 2 * j) for j in range(2, nz)]

    first, second = order_maps(plan)
    codes = call(
        bind(encode_kernel),
        [S((rows, w), jnp.int16)] * ni,
        [at, cont_value, first, second],
        [pltpu.VMEM((ni, rows, w), BF)] * 2,
        4 * pass_flops,
    )
    codes = exchange(codes, "inc", ni)
    quarter, _ = after(quarter, codes[1])
    pieces.insert(0, swap(quarter, "loc", nl, 2))

    hit = policy_maps(plan, asset_policy, inc)
    masses = call(
        bind(mass_kernel),
        [S((rows, w), BF)] * ni,
        [at, mass, hit, second],
        [pltpu.VMEM((ni, rows, w), BF)],
        3 * pass_flops,
    )
    mix_a, mix_b = call(
        bind(mix_kernel), [S((w, w), BF)] * 2, [trans_weight], specs=[VMEM]
    )
    masses, codes = after(masses, codes)
    masses = exchange(masses, "inc", ni)

    live = (live_mask > 0).astype(F32)[:, None]
    weights = call(
        bind(weight_kernel),
        [S((nz, packed, w), BF)],
        [at, *codes, mix_a, mix_b, live],
        [pltpu.VMEM((rows, w), jnp.int32)],
        3 * pass_flops,
    )
    weights, _ = after(weights[0], pieces)
    weights = along_z(weights)
    others = swap_core(weights)

    strip, _ = after(jnp.concatenate(pieces), masses)
    left, right = strip[:, : plan.cut], strip[:, plan.cut :]
    left = jnp.concatenate([left, swap(left, "inc", ni, 1)])
    right = jnp.concatenate([right, swap(right, "inc", ni, 2)])
    later_cost, _ = after(move_cost, (left, right))
    (own_near,) = call(
        bind(window_kernel),
        [S((rows, plan.window), BF)],
        [at, later_cost],
        [pltpu.VMEM((rows, ring), BF)],
    )
    near = [own_near, left, swap(left, "inc", ni, 2), right, swap(right, "inc", ni, 1)]
    near = near + [swap_core(x) for x in near]

    masses = call(bind(spread_kernel), [S((nz, rows, w), BF)], [at, *masses])
    masses, weights = after(masses[0], weights)
    masses = along_z(masses)

    totals, scaled, near = call(
        bind(total_kernel),
        [S((nz, packed, w), BF), S((nz, rows, w), BF), S((half, n), BF)],
        [at, weights, others, *near],
        [
            pltpu.VMEM((2, nz, packed, w), BF),
            pltpu.VMEM((n, w), BF),
            pltpu.VMEM((n, plan.window), BF),
            pltpu.VMEM((n, n), BF),
            pltpu.VMEM((nz, rows, w), F32),
            pltpu.SemaphoreType.DMA((3,)),
        ],
        solve_flops,
        specs=[SMEM, ANY, ANY] + [ANY] * len(near),
        out_specs=[VMEM, VMEM, ANY],
        vmem=46,
    )
    sent = along_z(totals)
    (share,) = call(
        bind(share_kernel), [S((nz, rows, w), BF)], [masses, totals], specs=[VMEM] * 2
    )
    movers = call(
        bind(mover_kernel),
        [S((rows, w), BF)] * nz,
        [at, share, swap_core(share), near, scaled],
        [
            pltpu.VMEM((nz, rows, w), BF),
            pltpu.VMEM((n, w), BF),
            pltpu.VMEM((half, n), BF),
            pltpu.SemaphoreType.DMA((nz,)),
        ],
        solve_flops,
        specs=[SMEM, VMEM, VMEM, ANY, VMEM],
    )
    close = [movers[0], swap(movers[1], "loc", nl, 2)]
    far = [swap(movers[2], "loc", nl, 4)]
    for j in range(3, nz):
        last, _ = after(movers[j], sent)
        far.append(swap(last, "loc", nl, 2 * j))

    pack = lambda part, outs, kernel: call(
        bind(kernel),
        outs,
        [at, mix_a, mix_b, *part],
        [pltpu.VMEM((packed, w), jnp.int32)],
        pass_flops,
    )
    close = pack(close, [S((packed, 2 * LANES), jnp.int16)] * ni, tail_kernel)
    close = exchange(close, "inc", ni)
    sent = call(bind(collect_kernel), [S((packed, w), BF)] * ni, [at, sent])
    sent = exchange(sent, "inc", ni)
    (new_value,) = call(
        bind(value_kernel),
        [S((rows, plan.columns), F32)],
        [at, *sent, hit, second, flow_util],
        [pltpu.VMEM((ni, packed, w), BF)],
        2 * pass_flops,
    )
    blocks, ready = close, (close, new_value)
    for part in far:
        part, _ = after(part, ready)
        ready = pack([part], [S((packed, LANES), jnp.int16)] * ni, tail_kernel)
        ready = exchange(ready, "inc", ni)
        blocks = blocks + ready

    (new_mass,) = call(
        bind(next_mass_kernel),
        [S((rows, plan.columns), F32)],
        [at, *blocks, first, second],
        [pltpu.VMEM((packed, w), jnp.int32)] + [pltpu.VMEM((ni, packed, w), BF)] * 2,
        4 * pass_flops,
    )
    return new_value, new_mass


def gathered(cont_value, flow_util, move_cost, live_mask, trans_weight, asset_policy, mass):
    high = lax.Precision.HIGHEST
    e, a = asset_policy.shape
    raised = trans_weight + 16.0 * jnp.eye(e, dtype=F32)
    trans_prob = raised / jnp.sum(raised, axis=1, keepdims=True)
    onehot = (asset_policy[:, :, None] == jnp.arange(a, dtype=jnp.int32)[None, None, :]).astype(F32)
    moved_rows = lax.all_to_all(cont_value, "inc", split_axis=0, concat_axis=1, tiled=True)
    expect = jnp.einsum("ef,jfb->jeb", trans_prob, moved_rows.reshape(-1, e, a), precision=high)
    chosen_all = jnp.einsum("jeb,eab->jea", expect, onehot, precision=high).reshape(-1, e * a)
    chosen = lax.all_to_all(chosen_all, "inc", split_axis=1, concat_axis=0, tiled=True)
    scores = DISCOUNT * chosen
    live_rows = live_mask[:, None] > 0
    local_max = jnp.max(jnp.where(live_rows, scores, F32(-1e30)), axis=0)
    column_max = lax.pmax(local_max, "loc")
    dest_weight = jnp.where(live_rows, jnp.exp(scores - column_max[None, :]), F32(0.0)).astype(BF)
    kernel = jnp.exp(-move_cost).astype(BF)
    totals = dot(kernel, lax.all_gather(dest_weight, "loc", axis=0, tiled=True))
    new_value = flow_util + column_max[None, :] + jnp.log(totals)
    shares = (mass / totals).astype(BF)
    arrived = lax.psum_scatter(
        lax.dot_general(
            kernel, shares, (((0,), (0,)), ((), ())), preferred_element_type=F32
        ).astype(BF),
        "loc",
        scatter_dimension=0,
        tiled=True,
    ).astype(F32)
    movers = dest_weight.astype(F32) * arrived
    moved_mass = lax.all_to_all(movers, "inc", split_axis=0, concat_axis=1, tiled=True)
    shuffled = jnp.einsum("jea,eab->jeb", moved_mass.reshape(-1, e, a), onehot, precision=high)
    mixed_mass = jnp.einsum("ef,jeb->jfb", trans_prob, shuffled, precision=high).reshape(-1, e * a)
    new_mass = lax.all_to_all(mixed_mass, "inc", split_axis=1, concat_axis=0, tiled=True)
    return new_value, new_mass


def solution(mesh):
    n_loc, n_inc = mesh.shape["loc"], mesh.shape["inc"]

    def shards(*args):
        rows, columns = args[0].shape
        plan = Plan(n_loc, n_inc, args[2].shape[1], rows, columns, *args[5].shape)
        if plan.fits():
            return state_split(plan, *args)
        return gathered(*args)

    split = P("loc", "inc")
    return jax.shard_map(
        shards,
        mesh=mesh,
        in_specs=(split, split, P("loc", None), P("loc"), P(), P(), split),
        out_specs=(split, split),
        check_vma=False,
    )
```

```python
import functools
import math

import jax
import jax.numpy as jnp
from jax import lax
from jax.experimental import pallas as pl
from jax.experimental.pallas import tpu as pltpu
from jax.sharding import PartitionSpec as P

DISCOUNT = 0.96
LANES = 128
TILE = 16
VALUE_LOW = -4.0
VALUE_HIGH = 252.0
STEP = (VALUE_HIGH - VALUE_LOW) / 65535.0
HALF = 32768.0
LN2 = math.log(2.0)
SCORE_STEP = DISCOUNT * STEP / LN2
SCORE_SHIFT = DISCOUNT * (HALF * STEP + VALUE_LOW)

BF = jnp.bfloat16
F32 = jnp.float32
VMEM = pl.BlockSpec(memory_space=pltpu.VMEM)
SMEM = pl.BlockSpec(memory_space=pltpu.SMEM)
ANY = pl.BlockSpec(memory_space=pl.ANY)


def dot(a, b):
    return lax.dot_general(a, b, (((1,), (0,)), ((), ())), preferred_element_type=F32)


def dot_nt(a, b):
    return lax.dot_general(a, b, (((1,), (1,)), ((), ())), preferred_element_type=F32)


def lanes_at(start, size):
    return pl.ds(pl.multiple_of(start, LANES), size)


def call(kernel, outs, ins, scratch=(), flops=0, specs=None, out_specs=None, vmem=24):
    moved = sum(math.prod(x.shape) * x.dtype.itemsize for x in list(ins) + list(outs))
    return pl.pallas_call(
        kernel,
        out_shape=tuple(outs),
        in_specs=specs or [SMEM] + [VMEM] * (len(ins) - 1),
        out_specs=tuple(out_specs or [VMEM] * len(outs)),
        scratch_shapes=list(scratch),
        compiler_params=pltpu.CompilerParams(vmem_limit_bytes=vmem * 1024 * 1024),
        cost_estimate=pl.CostEstimate(flops=flops, bytes_accessed=moved, transcendentals=0),
    )(*ins)


class Plan:
    def __init__(self, n_loc, n_inc, counties, rows, columns, incomes, assets):
        self.n_loc, self.n_inc, self.n_z = n_loc, n_inc, n_loc // 2
        self.counties, self.rows, self.columns = counties, rows, columns
        self.incomes, self.assets = incomes, assets
        self.own_incomes = incomes // n_inc
        self.own_assets = assets // n_inc
        self.group_assets = LANES // self.own_incomes
        self.wide = n_inc * LANES
        self.packed = rows + TILE
        self.half = counties // 2
        self.block_rows = counties // LANES
        self.window = (self.block_rows // 2 + 1) * LANES
        self.stride = rows // n_inc // TILE * TILE
        self.quarter = rows - self.stride * (n_inc - 1)
        self.cut = (self.window // LANES + 1) // 2 * LANES

    def fits(self):
        power = lambda n: n > 1 and n & (n - 1) == 0
        return (
            power(self.n_loc)
            and power(self.n_z)
            and power(self.n_inc)
            and self.incomes == LANES
            and self.own_incomes * self.group_assets == LANES
            and self.columns == self.n_z * self.wide
            and self.n_z == self.n_inc == 4
            and self.own_assets == self.n_z * self.group_assets
            and self.rows % TILE == 0
            and self.counties == self.rows * self.n_loc
            and self.counties % LANES == 0
            and self.block_rows % 2 == 1
        )


def order_maps(plan):
    w, oa, oi = plan.wide, plan.own_assets, plan.own_incomes
    r = lax.broadcasted_iota(jnp.int32, (w, w), 0)
    c = lax.broadcasted_iota(jnp.int32, (w, w), 1)
    a = plan.assets
    spot = (r % a) // oa * LANES + r // a * oa + r % oa
    first = (c == spot).astype(BF)
    second = (c == r % oa * oi + r // oa).astype(BF)
    return first, second


def encode_kernel(plan, at, value, first, second, *refs):
    outs, (high, low) = refs[: plan.n_inc], refs[plan.n_inc :]
    inc, w = at[1], plan.wide
    for t in range(plan.n_inc):
        x = value[:, t * w : (t + 1) * w]
        code = jnp.clip(jnp.round((x - VALUE_LOW) * (1.0 / STEP)) - HALF, -HALF, HALF - 1.0)
        top = jnp.floor(code * (1.0 / 256.0))
        rest = code - 256.0 * top
        moved_top = dot(top.astype(BF), first[...]).astype(BF)
        moved_rest = dot(rest.astype(BF), first[...]).astype(BF)
        for q in range(plan.n_inc):
            high[q, :, t * LANES : (t + 1) * LANES] = moved_top[:, q * LANES : (q + 1) * LANES]
            low[q, :, t * LANES : (t + 1) * LANES] = moved_rest[:, q * LANES : (q + 1) * LANES]
    for k in range(plan.n_inc):
        q = inc ^ k
        code = dot(high[q], second[...]) * 256.0 + dot(low[q], second[...])
        outs[k][...] = code.astype(jnp.int32).astype(jnp.int16)


def weight_kernel(plan, at, *refs):
    ni, nz, rows = plan.n_inc, plan.n_z, plan.rows
    codes, (mix_a, mix_b, live), refs = refs[:ni], refs[ni : ni + 3], refs[ni + 3 :]
    weights, held = refs
    inc, w = at[1], plan.wide
    alive = live[...] > 0.0
    for g in range(nz):
        for k in range(ni):
            held[:, lanes_at((inc ^ k) * LANES, LANES)] = codes[k][
                :, g * LANES : (g + 1) * LANES
            ].astype(jnp.int32)
        code = held[...]
        top = (code >> 8).astype(F32).astype(BF)
        rest = (code & 255).astype(F32).astype(BF)
        mixed = (dot(top, mix_a[...]) + dot(top, mix_b[...])) * 256.0 + dot(rest, mix_a[...])
        score = mixed * SCORE_STEP
        peak = jnp.max(jnp.where(alive, score, -512.0), axis=0, keepdims=True)
        peak = jnp.ceil(peak)
        weights[g, 0:rows, :] = jnp.where(alive, jnp.exp2(score - peak), 0.0).astype(BF)
        weights[g, rows:, :] = jnp.broadcast_to(peak, (TILE, w)).astype(BF)


def mass_kernel(plan, at, mass, hit, second, *refs):
    outs, (held,) = refs[: plan.n_inc], refs[plan.n_inc :]
    inc, w = at[1], plan.wide
    for t in range(plan.n_inc):
        x = mass[:, t * w : (t + 1) * w]
        top = x.astype(BF)
        rest = (x - top.astype(F32)).astype(BF)
        moved = (dot(top, hit[t]) + dot(rest, hit[t])).astype(BF)
        for q in range(plan.n_inc):
            held[q, :, t * LANES : (t + 1) * LANES] = moved[:, q * LANES : (q + 1) * LANES]
    for k in range(plan.n_inc):
        outs[k][...] = dot(held[inc ^ k], second[...]).astype(BF)


def spread_kernel(plan, at, *refs):
    *ins, out = refs
    for k in range(plan.n_inc):
        for g in range(plan.n_z):
            out[g, :, lanes_at((at[1] ^ k) * LANES, LANES)] = ins[k][
                :, g * LANES : (g + 1) * LANES
            ]


def collect_kernel(plan, at, *refs):
    blocks, *outs = refs
    for k in range(plan.n_inc):
        for g in range(plan.n_z):
            outs[k][:, g * LANES : (g + 1) * LANES] = blocks[
                g, :, lanes_at((at[1] ^ k) * LANES, LANES)
            ]


def windows(plan, start, count, near, held, out):
    n = plan.counties
    held[:, :n] = near
    held[:, n:] = near[:, : plan.window - LANES]
    for g in range(count // TILE):
        block = (start + g * TILE) // LANES
        out[g * TILE : (g + 1) * TILE, :] = held[
            g * TILE : (g + 1) * TILE, lanes_at(block * LANES, plan.window)
        ]


def quarter_kernel(plan, at, cost, out, part, held, sem):
    start = pl.multiple_of(at[1] * plan.stride, TILE)
    copy = pltpu.make_async_copy(cost.at[pl.ds(start, plan.quarter)], part, sem)
    copy.start()
    copy.wait()
    near = jnp.exp(-part[...]).astype(BF)
    windows(plan, at[0] * plan.rows + start, plan.quarter, near, held, out)


def window_kernel(plan, at, cost, out, held):
    near = jnp.exp(-cost[...]).astype(BF)
    windows(plan, at[0] * plan.rows, plan.rows, near, held, out)


def county_rows(plan, at, z, side):
    start = (2 * z + ((at[0] % 2) ^ side)) * plan.rows
    return pl.ds(pl.multiple_of(start, TILE), plan.rows)


def near_copies(plan, near, held, sems):
    blocks = [pl.ds(j * plan.rows, plan.rows) for j in range(plan.n_z)]
    return [
        pltpu.make_async_copy(near.at[b], held.at[b], sems.at[j]) for j, b in enumerate(blocks)
    ]


def total_kernel(plan, at, *refs):
    nz, rows, cut = plan.n_z, plan.rows, plan.cut
    own_weights, other_weights, refs = refs[0], refs[1], refs[2:]
    both, (sent, scaled, near, given, weight, strip, full, sums, sems) = refs[:10], refs[10:]
    z, core, inc = at[0] // 2, at[0] % 2, at[1]
    left, right = pl.ds(0, cut), pl.ds(cut, plan.window - cut)
    always = []
    for side in range(2):
        own, *parts = both[side * 5 : side * 5 + 5]
        first_row = lambda j: (2 * (z ^ j) + (core ^ side)) * rows
        here = pl.ds(pl.multiple_of(first_row(0), TILE), rows)
        for half, lanes in enumerate((left, right)):
            always.append((half, None, own.at[:, lanes], strip.at[here, lanes]))
        places = ((0, 1), left), ((2, 3), left), ((0, 2), right), ((1, 3), right)
        for part, (steps, lanes) in zip(parts, places):
            for h, k in enumerate(steps):
                q = inc ^ k
                for j in range(1, nz):
                    base = (h * (nz - 1) + j - 1) * plan.quarter
                    start = first_row(j) + q * plan.stride
                    rest = plan.quarter - plan.stride
                    to = lambda r, size: strip.at[pl.ds(pl.multiple_of(r, TILE), size), lanes]
                    half = int(lanes is right)
                    always.append((half, None, part.at[pl.ds(base, plan.stride)], to(start, plan.stride)))
                    extra, when = part.at[pl.ds(base + plan.stride, rest)], q == plan.n_inc - 1
                    always.append((half, when, extra, to(start + plan.stride, rest)))
    loads = [pltpu.make_async_copy(own_weights, given.at[0], sems.at[0])]
    loads.append(pltpu.make_async_copy(other_weights, given.at[1], sems.at[0]))
    for c in loads:
        c.start()
    copies = [[], []]
    for half, when, a, b in always:
        copies[half].append((when, pltpu.make_async_copy(a, b, sems.at[1 + half])))
    for when, c in copies[0] + copies[1]:
        pl.when(when)(c.start) if when is not None else c.start()

    for c in loads:
        c.wait()
    places = [(side, g) for side in range(2) for g in range(nz)]
    peaks = [given[side, g, rows : rows + 1, :].astype(F32) for side, g in places]
    peak = functools.reduce(jnp.maximum, peaks)
    for (side, g), own_peak in zip(places, peaks):
        part = (given[side, g, :rows, :].astype(F32) * jnp.exp2(own_peak - peak)).astype(BF)
        weight[county_rows(plan, at, g, side), :] = part
        if side == 0:
            scaled[g] = part

    blocks, cuts = plan.block_rows, (0, cut // LANES, plan.window // LANES)
    for half in range(2):
        for when, c in copies[half]:
            pl.when(when)(c.wait) if when is not None else c.wait()
        for i in range(blocks):
            for k in range(cuts[half], cuts[half + 1]):
                j = (i + k) % blocks
                tile = strip[i * LANES : (i + 1) * LANES, k * LANES : (k + 1) * LANES]
                full[i * LANES : (i + 1) * LANES, j * LANES : (j + 1) * LANES] = tile
                if k:
                    full[j * LANES : (j + 1) * LANES, i * LANES : (i + 1) * LANES] = tile.T
    copies = []
    for j in range(nz):
        out = near.at[pl.ds(j * rows, rows)]
        copies.append(
            pltpu.make_async_copy(full.at[county_rows(plan, at, j, 0)], out, sems.at[0])
        )
    for c in copies:
        c.start()
    def product(j, carry):
        sums[j] = dot(full[county_rows(plan, at, j, 0), :], weight[...])
        return carry

    lax.fori_loop(0, nz, product, 0)
    sent[:, :rows, :] = sums[...].astype(BF)
    sent[:, rows:, :] = jnp.broadcast_to(peak[None], (nz, TILE, plan.wide)).astype(BF)
    for c in copies:
        c.wait()


def share_kernel(plan, masses, totals, out):
    for g in range(plan.n_z):
        total = totals[g, : plan.rows, :].astype(F32)
        out[g] = (masses[g].astype(F32) / total).astype(BF)


def mover_kernel(plan, at, own, other, near, scaled, *refs):
    nz, rows = plan.n_z, plan.rows
    outs, (movers, share, held, sems) = refs[:nz], refs[nz:]
    copies = near_copies(plan, near, held, sems)
    for c in copies:
        c.start()
    for side, x in enumerate((own, other)):
        for g in range(nz):
            share[county_rows(plan, at, g, side), :] = x[g]
    for g in range(nz):
        copies[g].wait()
        arrived = dot(held[g * rows : (g + 1) * rows, :], share[...])
        movers[g] = (scaled[g].astype(F32) * arrived).astype(BF)
    for j in range(nz):
        outs[j][...] = movers[(at[0] // 2) ^ j]


def code_blocks(plan, mix_a, mix_b, ins, mixed):
    rows = plan.rows
    for i, part in enumerate(ins):
        x = part[...]
        new = dot_nt(x, mix_a[...]) + dot_nt(x, mix_b[...])
        most = jnp.maximum(jnp.max(new, axis=0, keepdims=True), 1e-30)
        power = jnp.ceil(jnp.log2(most))
        code = jnp.minimum(jnp.round(new * jnp.exp2(15.0 - power)), HALF - 1.0)
        mixed[:rows, :] = code.astype(jnp.int32)
        mixed[rows:, :] = jnp.broadcast_to(power, (TILE, plan.wide)).astype(jnp.int32)
        yield i


def tail_kernel(plan, at, mix_a, mix_b, *refs):
    ins, outs, mixed = refs[: -1 - plan.n_inc], refs[-1 - plan.n_inc : -1], refs[-1]
    for i in code_blocks(plan, mix_a, mix_b, ins, mixed):
        for k in range(plan.n_inc):
            block = mixed[:, lanes_at((at[1] ^ k) * LANES, LANES)].astype(jnp.int16)
            outs[k][:, i * LANES : (i + 1) * LANES] = block


def next_mass_kernel(plan, at, *refs):
    ni, w, rows = plan.n_inc, plan.wide, plan.rows
    ins, (first, second, out, held, high, low, done, sem) = refs[:-8], refs[-8:]
    copies = []
    z, inc = at[0] // 2, at[1]
    for k in range(ni):
        j = 0
        for part in ins[k::ni]:
            for i in range(part.shape[1] // LANES):
                held[:, lanes_at((z ^ j) * LANES, LANES)] = part[
                    :, i * LANES : (i + 1) * LANES
                ].astype(jnp.int32)
                j += 1
        code = held[...]
        for part, into in ((code >> 8, high), (code & 255, low)):
            back = dot_nt(part.astype(F32).astype(BF), second[...]).astype(BF)
            for t in range(ni):
                into[t, :, lanes_at((inc ^ k) * LANES, LANES)] = back[:, t * LANES : (t + 1) * LANES]
    for t in range(ni):
        code = dot_nt(high[t], first[...]) * 256.0 + dot_nt(low[t], first[...])
        done[t] = code[:rows, :] * jnp.exp2(code[rows : rows + 1, :] - 15.0)
        copies.append(pltpu.make_async_copy(done.at[t], out.at[:, pl.ds(t * w, w)], sem))
        copies[t].start()
    for c in copies:
        c.wait()


def value_kernel(plan, at, *refs):
    ni, w, rows = plan.n_inc, plan.wide, plan.rows
    ins, (hit, second, flow), (out, held) = refs[:ni], refs[ni : ni + 3], refs[ni + 3 :]
    inc = at[1]
    for k in range(ni):
        back = dot_nt(ins[k][...], second[...]).astype(BF)
        for t in range(ni):
            held[t, :, lanes_at((inc ^ k) * LANES, LANES)] = back[:, t * LANES : (t + 1) * LANES]
    for t in range(ni):
        got = dot_nt(held[t], hit[t])
        peak = got[rows : rows + 1, :] * LN2 + SCORE_SHIFT
        out[:, t * w : (t + 1) * w] = flow[:, t * w : (t + 1) * w] + (peak + jnp.log(got[:rows, :]))


def mix_kernel(plan, trans, out_a, out_b):
    e, oi, ga, w = plan.incomes, plan.own_incomes, plan.group_assets, plan.wide
    grid = lambda shape, axis: lax.broadcasted_iota(jnp.int32, shape, axis)
    raised = trans[...] + jnp.where(grid((e, e), 0) == grid((e, e), 1), 16.0, 0.0)
    prob = (raised / jnp.sum(raised, axis=1, keepdims=True)).T
    lane = grid((e, w), 1)
    place = (grid((e, w), 0) == lane // LANES * oi + lane % oi).astype(BF)
    same = grid((w, w), 0) // oi % ga == grid((w, w), 1) // oi % ga
    top = prob.astype(BF)
    for part, out in ((top, out_a), ((prob - top.astype(F32)).astype(BF), out_b)):
        wide = dot(part, place)
        blocks = [wide[i * oi : (i + 1) * oi] for i in range(plan.n_inc) for _ in range(ga)]
        out[...] = jnp.where(same, jnp.concatenate(blocks, axis=0), 0.0).astype(BF)


def policy_maps(plan, asset_policy, inc):
    ni, oa, a, w = plan.n_inc, plan.own_assets, plan.assets, plan.wide
    own = lax.dynamic_slice_in_dim(asset_policy, inc * plan.own_incomes, plan.own_incomes, 0)
    group = w // a
    row_income = jnp.arange(group, dtype=jnp.int32)[None, :, None]
    own = own.reshape(ni, group, a)
    lane = own // oa * LANES + row_income * oa + own % oa
    lane = lane.reshape(ni, w, 1)
    return (lane == lax.broadcasted_iota(jnp.int32, (ni, w, w), 2)).astype(BF)


def swap(x, axis, n, k):
    return lax.ppermute(x, axis, [(s, s ^ k) for s in range(n)]) if k else x


def exchange(blocks, axis, n, unit=1):
    got = {k: swap(blocks[k], axis, n, k * unit) for k in reversed(range(len(blocks)))}
    return [got[k] for k in range(len(blocks))]


def after(x, y):
    return lax.optimization_barrier((x, y))


def state_split(plan, cont_value, flow_util, move_cost, live_mask, trans_weight, asset_policy, mass):
    ni, nl, nz, rows, n = plan.n_inc, plan.n_loc, plan.n_z, plan.rows, plan.counties
    w, packed, half = plan.wide, plan.packed, plan.half
    S = jax.ShapeDtypeStruct
    loc, inc = lax.axis_index("loc"), lax.axis_index("inc")
    at = jnp.stack([loc, inc]).astype(jnp.int32)
    bind = lambda f: functools.partial(f, plan)
    pass_flops = 2 * rows * plan.columns * w
    solve_flops = 2 * half * n * w
    swap_core = lambda x: swap(x, "loc", nl, 1)
    lines = [list(range(core, nl, 2)) for core in range(2)]
    along_z = lambda x: lax.all_to_all(x, "loc", 0, 0, axis_index_groups=lines)
    ring = n + plan.window - LANES

    (quarter,) = call(
        bind(quarter_kernel),
        [S((plan.quarter, plan.window), BF)],
        [at, move_cost],
        [
            pltpu.VMEM((plan.quarter, n), F32),
            pltpu.VMEM((plan.quarter, ring), BF),
            pltpu.SemaphoreType.DMA,
        ],
        specs=[SMEM, ANY],
    )
    pieces = [swap(quarter, "loc", nl, 2 * j) for j in range(2, nz)]

    first, second = order_maps(plan)
    codes = call(
        bind(encode_kernel),
        [S((rows, w), jnp.int16)] * ni,
        [at, cont_value, first, second],
        [pltpu.VMEM((ni, rows, w), BF)] * 2,
        4 * pass_flops,
    )
    codes = exchange(codes, "inc", ni)
    quarter, _ = after(quarter, codes[1])
    pieces.insert(0, swap(quarter, "loc", nl, 2))

    hit = policy_maps(plan, asset_policy, inc)
    masses = call(
        bind(mass_kernel),
        [S((rows, w), BF)] * ni,
        [at, mass, hit, second],
        [pltpu.VMEM((ni, rows, w), BF)],
        3 * pass_flops,
    )
    mix_a, mix_b = call(
        bind(mix_kernel), [S((w, w), BF)] * 2, [trans_weight], specs=[VMEM]
    )
    masses, codes = after(masses, codes)
    masses = exchange(masses, "inc", ni)

    live = (live_mask > 0).astype(F32)[:, None]
    weights = call(
        bind(weight_kernel),
        [S((nz, packed, w), BF)],
        [at, *codes, mix_a, mix_b, live],
        [pltpu.VMEM((rows, w), jnp.int32)],
        3 * pass_flops,
    )
    weights, _ = after(weights[0], pieces)
    weights = along_z(weights)
    others = swap_core(weights)

    strip, _ = after(jnp.concatenate(pieces), masses)
    left, right = strip[:, : plan.cut], strip[:, plan.cut :]
    left = jnp.concatenate([left, swap(left, "inc", ni, 1)])
    right = jnp.concatenate([right, swap(right, "inc", ni, 2)])
    later_cost, _ = after(move_cost, (left, right))
    (own_near,) = call(
        bind(window_kernel),
        [S((rows, plan.window), BF)],
        [at, later_cost],
        [pltpu.VMEM((rows, ring), BF)],
    )
    near = [own_near, left, swap(left, "inc", ni, 2), right, swap(right, "inc", ni, 1)]
    near = near + [swap_core(x) for x in near]

    masses = call(bind(spread_kernel), [S((nz, rows, w), BF)], [at, *masses])
    masses, weights = after(masses[0], weights)
    masses = along_z(masses)

    totals, scaled, near = call(
        bind(total_kernel),
        [S((nz, packed, w), BF), S((nz, rows, w), BF), S((half, n), BF)],
        [at, weights, others, *near],
        [
            pltpu.VMEM((2, nz, packed, w), BF),
            pltpu.VMEM((n, w), BF),
            pltpu.VMEM((n, plan.window), BF),
            pltpu.VMEM((n, n), BF),
            pltpu.VMEM((nz, rows, w), F32),
            pltpu.SemaphoreType.DMA((3,)),
        ],
        solve_flops,
        specs=[SMEM, ANY, ANY] + [ANY] * len(near),
        out_specs=[VMEM, VMEM, ANY],
        vmem=46,
    )
    sent = along_z(totals)
    (share,) = call(
        bind(share_kernel), [S((nz, rows, w), BF)], [masses, totals], specs=[VMEM] * 2
    )
    movers = call(
        bind(mover_kernel),
        [S((rows, w), BF)] * nz,
        [at, share, swap_core(share), near, scaled],
        [
            pltpu.VMEM((nz, rows, w), BF),
            pltpu.VMEM((n, w), BF),
            pltpu.VMEM((half, n), BF),
            pltpu.SemaphoreType.DMA((nz,)),
        ],
        solve_flops,
        specs=[SMEM, VMEM, VMEM, ANY, VMEM],
        vmem=56,
    )
    close = [movers[0], swap(movers[1], "loc", nl, 2)]
    far = [swap(movers[2], "loc", nl, 4)]
    for j in range(3, nz):
        last, _ = after(movers[j], sent)
        far.append(swap(last, "loc", nl, 2 * j))

    pack = lambda part, outs, kernel: call(
        bind(kernel),
        outs,
        [at, mix_a, mix_b, *part],
        [pltpu.VMEM((packed, w), jnp.int32)],
        pass_flops,
    )
    close = pack(close, [S((packed, 2 * LANES), jnp.int16)] * ni, tail_kernel)
    close = exchange(close, "inc", ni)
    sent = call(bind(collect_kernel), [S((packed, w), BF)] * ni, [at, sent])
    sent = exchange(sent, "inc", ni)
    (new_value,) = call(
        bind(value_kernel),
        [S((rows, plan.columns), F32)],
        [at, *sent, hit, second, flow_util],
        [pltpu.VMEM((ni, packed, w), BF)],
        2 * pass_flops,
    )
    blocks, ready = close, (close, new_value)
    for part in far:
        part, _ = after(part, ready)
        ready = pack([part], [S((packed, LANES), jnp.int16)] * ni, tail_kernel)
        ready = exchange(ready, "inc", ni)
        blocks = blocks + ready

    (new_mass,) = call(
        bind(next_mass_kernel),
        [S((rows, plan.columns), F32)],
        [at, *blocks, first, second],
        [pltpu.VMEM((packed, w), jnp.int32)]
        + [pltpu.VMEM((ni, packed, w), BF)] * 2
        + [pltpu.VMEM((ni, rows, w), F32), pltpu.SemaphoreType.DMA],
        4 * pass_flops,
        out_specs=[ANY],
    )
    return new_value, new_mass


def gathered(cont_value, flow_util, move_cost, live_mask, trans_weight, asset_policy, mass):
    high = lax.Precision.HIGHEST
    e, a = asset_policy.shape
    raised = trans_weight + 16.0 * jnp.eye(e, dtype=F32)
    trans_prob = raised / jnp.sum(raised, axis=1, keepdims=True)
    onehot = (asset_policy[:, :, None] == jnp.arange(a, dtype=jnp.int32)[None, None, :]).astype(F32)
    moved_rows = lax.all_to_all(cont_value, "inc", split_axis=0, concat_axis=1, tiled=True)
    expect = jnp.einsum("ef,jfb->jeb", trans_prob, moved_rows.reshape(-1, e, a), precision=high)
    chosen_all = jnp.einsum("jeb,eab->jea", expect, onehot, precision=high).reshape(-1, e * a)
    chosen = lax.all_to_all(chosen_all, "inc", split_axis=1, concat_axis=0, tiled=True)
    scores = DISCOUNT * chosen
    live_rows = live_mask[:, None] > 0
    local_max = jnp.max(jnp.where(live_rows, scores, F32(-1e30)), axis=0)
    column_max = lax.pmax(local_max, "loc")
    dest_weight = jnp.where(live_rows, jnp.exp(scores - column_max[None, :]), F32(0.0)).astype(BF)
    kernel = jnp.exp(-move_cost).astype(BF)
    totals = dot(kernel, lax.all_gather(dest_weight, "loc", axis=0, tiled=True))
    new_value = flow_util + column_max[None, :] + jnp.log(totals)
    shares = (mass / totals).astype(BF)
    arrived = lax.psum_scatter(
        lax.dot_general(
            kernel, shares, (((0,), (0,)), ((), ())), preferred_element_type=F32
        ).astype(BF),
        "loc",
        scatter_dimension=0,
        tiled=True,
    ).astype(F32)
    movers = dest_weight.astype(F32) * arrived
    moved_mass = lax.all_to_all(movers, "inc", split_axis=0, concat_axis=1, tiled=True)
    shuffled = jnp.einsum("jea,eab->jeb", moved_mass.reshape(-1, e, a), onehot, precision=high)
    mixed_mass = jnp.einsum("ef,jeb->jfb", trans_prob, shuffled, precision=high).reshape(-1, e * a)
    new_mass = lax.all_to_all(mixed_mass, "inc", split_axis=1, concat_axis=0, tiled=True)
    return new_value, new_mass


def solution(mesh):
    n_loc, n_inc = mesh.shape["loc"], mesh.shape["inc"]

    def shards(*args):
        rows, columns = args[0].shape
        plan = Plan(n_loc, n_inc, args[2].shape[1], rows, columns, *args[5].shape)
        if plan.fits():
            return state_split(plan, *args)
        return gathered(*args)

    split = P("loc", "inc")
    return jax.shard_map(
        shards,
        mesh=mesh,
        in_specs=(split, split, P("loc", None), P("loc"), P(), P(), split),
        out_specs=(split, split),
        check_vma=False,
    )
```

```python
import functools
import math

import jax
import jax.numpy as jnp
from jax import lax
from jax.experimental import pallas as pl
from jax.experimental.pallas import tpu as pltpu
from jax.sharding import PartitionSpec as P

DISCOUNT = 0.96
LANES = 128
TILE = 16
VALUE_LOW = -4.0
VALUE_HIGH = 252.0
STEP = (VALUE_HIGH - VALUE_LOW) / 65535.0
HALF = 32768.0
LN2 = math.log(2.0)
SCORE_STEP = DISCOUNT * STEP / LN2
SCORE_SHIFT = DISCOUNT * (HALF * STEP + VALUE_LOW)

BF = jnp.bfloat16
F32 = jnp.float32
VMEM = pl.BlockSpec(memory_space=pltpu.VMEM)
SMEM = pl.BlockSpec(memory_space=pltpu.SMEM)
ANY = pl.BlockSpec(memory_space=pl.ANY)


def dot(a, b):
    return lax.dot_general(a, b, (((1,), (0,)), ((), ())), preferred_element_type=F32)


def dot_nt(a, b):
    return lax.dot_general(a, b, (((1,), (1,)), ((), ())), preferred_element_type=F32)


def lanes_at(start, size):
    return pl.ds(pl.multiple_of(start, LANES), size)


def call(kernel, outs, ins, scratch=(), flops=0, specs=None, out_specs=None, vmem=24):
    moved = sum(math.prod(x.shape) * x.dtype.itemsize for x in list(ins) + list(outs))
    return pl.pallas_call(
        kernel,
        out_shape=tuple(outs),
        in_specs=specs or [SMEM] + [VMEM] * (len(ins) - 1),
        out_specs=tuple(out_specs or [VMEM] * len(outs)),
        scratch_shapes=list(scratch),
        compiler_params=pltpu.CompilerParams(vmem_limit_bytes=vmem * 1024 * 1024),
        cost_estimate=pl.CostEstimate(flops=flops, bytes_accessed=moved, transcendentals=0),
    )(*ins)


class Plan:
    def __init__(self, n_loc, n_inc, counties, rows, columns, incomes, assets):
        self.n_loc, self.n_inc, self.n_z = n_loc, n_inc, n_loc // 2
        self.counties, self.rows, self.columns = counties, rows, columns
        self.incomes, self.assets = incomes, assets
        self.own_incomes = incomes // n_inc
        self.own_assets = assets // n_inc
        self.group_assets = LANES // self.own_incomes
        self.wide = n_inc * LANES
        self.packed = rows + TILE
        self.half = counties // 2
        self.block_rows = counties // LANES
        self.window = (self.block_rows // 2 + 1) * LANES
        self.stride = rows // n_inc // TILE * TILE
        self.quarter = rows - self.stride * (n_inc - 1)
        self.cut = (self.window // LANES + 1) // 2 * LANES

    def fits(self):
        power = lambda n: n > 1 and n & (n - 1) == 0
        return (
            power(self.n_loc)
            and power(self.n_z)
            and power(self.n_inc)
            and self.incomes == LANES
            and self.own_incomes * self.group_assets == LANES
            and self.columns == self.n_z * self.wide
            and self.n_z == self.n_inc == 4
            and self.own_assets == self.n_z * self.group_assets
            and self.rows % TILE == 0
            and self.counties == self.rows * self.n_loc
            and self.counties % LANES == 0
            and self.block_rows % 2 == 1
        )


def order_maps(plan):
    w, oa, oi = plan.wide, plan.own_assets, plan.own_incomes
    r = lax.broadcasted_iota(jnp.int32, (w, w), 0)
    c = lax.broadcasted_iota(jnp.int32, (w, w), 1)
    a = plan.assets
    spot = (r % a) // oa * LANES + r // a * oa + r % oa
    first = (c == spot).astype(BF)
    second = (c == r % oa * oi + r // oa).astype(BF)
    return first, second


def encode_kernel(plan, at, value, first, second, *refs):
    outs, (high, low) = refs[: plan.n_inc], refs[plan.n_inc :]
    inc, w = at[1], plan.wide
    for t in range(plan.n_inc):
        x = value[:, t * w : (t + 1) * w]
        code = jnp.clip(jnp.round((x - VALUE_LOW) * (1.0 / STEP)) - HALF, -HALF, HALF - 1.0)
        top = jnp.floor(code * (1.0 / 256.0))
        rest = code - 256.0 * top
        moved_top = dot(top.astype(BF), first[...]).astype(BF)
        moved_rest = dot(rest.astype(BF), first[...]).astype(BF)
        for q in range(plan.n_inc):
            high[q, :, t * LANES : (t + 1) * LANES] = moved_top[:, q * LANES : (q + 1) * LANES]
            low[q, :, t * LANES : (t + 1) * LANES] = moved_rest[:, q * LANES : (q + 1) * LANES]
    for k in range(plan.n_inc):
        q = inc ^ k
        code = dot(high[q], second[...]) * 256.0 + dot(low[q], second[...])
        outs[k][...] = code.astype(jnp.int32).astype(jnp.int16)


def weight_kernel(plan, at, *refs):
    ni, nz, rows = plan.n_inc, plan.n_z, plan.rows
    codes, (mix_a, mix_b, live), refs = refs[:ni], refs[ni : ni + 3], refs[ni + 3 :]
    weights, held = refs
    inc, w = at[1], plan.wide
    alive = live[...] > 0.0
    for g in range(nz):
        for k in range(ni):
            held[:, lanes_at((inc ^ k) * LANES, LANES)] = codes[k][
                :, g * LANES : (g + 1) * LANES
            ].astype(jnp.int32)
        code = held[...]
        top = (code >> 8).astype(F32).astype(BF)
        rest = (code & 255).astype(F32).astype(BF)
        mixed = (dot(top, mix_a[...]) + dot(top, mix_b[...])) * 256.0 + dot(rest, mix_a[...])
        score = mixed * SCORE_STEP
        peak = jnp.max(jnp.where(alive, score, -512.0), axis=0, keepdims=True)
        peak = jnp.ceil(peak)
        weights[g, 0:rows, :] = jnp.where(alive, jnp.exp2(score - peak), 0.0).astype(BF)
        weights[g, rows:, :] = jnp.broadcast_to(peak, (TILE, w)).astype(BF)


def mass_kernel(plan, at, mass, hit, second, *refs):
    outs, (held,) = refs[: plan.n_inc], refs[plan.n_inc :]
    inc, w = at[1], plan.wide
    for t in range(plan.n_inc):
        x = mass[:, t * w : (t + 1) * w]
        top = x.astype(BF)
        rest = (x - top.astype(F32)).astype(BF)
        moved = (dot(top, hit[t]) + dot(rest, hit[t])).astype(BF)
        for q in range(plan.n_inc):
            held[q, :, t * LANES : (t + 1) * LANES] = moved[:, q * LANES : (q + 1) * LANES]
    for k in range(plan.n_inc):
        outs[k][...] = dot(held[inc ^ k], second[...]).astype(BF)


def spread_kernel(plan, at, *refs):
    *ins, out = refs
    for k in range(plan.n_inc):
        for g in range(plan.n_z):
            out[g, :, lanes_at((at[1] ^ k) * LANES, LANES)] = ins[k][
                :, g * LANES : (g + 1) * LANES
            ]


def collect_kernel(plan, at, *refs):
    blocks, *outs = refs
    for k in range(plan.n_inc):
        for g in range(plan.n_z):
            outs[k][:, g * LANES : (g + 1) * LANES] = blocks[
                g, :, lanes_at((at[1] ^ k) * LANES, LANES)
            ]


def windows(plan, start, count, near, held, out):
    n = plan.counties
    held[:, :n] = near
    held[:, n:] = near[:, : plan.window - LANES]
    for g in range(count // TILE):
        block = (start + g * TILE) // LANES
        out[g * TILE : (g + 1) * TILE, :] = held[
            g * TILE : (g + 1) * TILE, lanes_at(block * LANES, plan.window)
        ]


def quarter_kernel(plan, at, cost, out, part, held, sem):
    start = pl.multiple_of(at[1] * plan.stride, TILE)
    copy = pltpu.make_async_copy(cost.at[pl.ds(start, plan.quarter)], part, sem)
    copy.start()
    copy.wait()
    near = jnp.exp(-part[...]).astype(BF)
    windows(plan, at[0] * plan.rows + start, plan.quarter, near, held, out)


def window_kernel(plan, at, cost, out, held):
    near = jnp.exp(-cost[...]).astype(BF)
    windows(plan, at[0] * plan.rows, plan.rows, near, held, out)


def county_rows(plan, at, z, side):
    start = (2 * z + ((at[0] % 2) ^ side)) * plan.rows
    return pl.ds(pl.multiple_of(start, TILE), plan.rows)


def near_copies(plan, near, held, sems):
    blocks = [pl.ds(j * plan.rows, plan.rows) for j in range(plan.n_z)]
    return [
        pltpu.make_async_copy(near.at[b], held.at[b], sems.at[j]) for j, b in enumerate(blocks)
    ]


def total_kernel(plan, at, *refs):
    nz, rows, cut = plan.n_z, plan.rows, plan.cut
    own_weights, other_weights, refs = refs[0], refs[1], refs[2:]
    both, (sent, scaled_out, near, given, scaled, weight, strip, full, sums, sems) = refs[:10], refs[10:]
    z, core, inc = at[0] // 2, at[0] % 2, at[1]
    left, right = pl.ds(0, cut), pl.ds(cut, plan.window - cut)
    always = []
    for side in range(2):
        own, *parts = both[side * 5 : side * 5 + 5]
        first_row = lambda j: (2 * (z ^ j) + (core ^ side)) * rows
        here = pl.ds(pl.multiple_of(first_row(0), TILE), rows)
        for half, lanes in enumerate((left, right)):
            always.append((half, None, own.at[:, lanes], strip.at[here, lanes]))
        places = ((0, 1), left), ((2, 3), left), ((0, 2), right), ((1, 3), right)
        for part, (steps, lanes) in zip(parts, places):
            for h, k in enumerate(steps):
                q = inc ^ k
                for j in range(1, nz):
                    base = (h * (nz - 1) + j - 1) * plan.quarter
                    start = first_row(j) + q * plan.stride
                    rest = plan.quarter - plan.stride
                    to = lambda r, size: strip.at[pl.ds(pl.multiple_of(r, TILE), size), lanes]
                    half = int(lanes is right)
                    always.append((half, None, part.at[pl.ds(base, plan.stride)], to(start, plan.stride)))
                    extra, when = part.at[pl.ds(base + plan.stride, rest)], q == plan.n_inc - 1
                    always.append((half, when, extra, to(start + plan.stride, rest)))
    loads = [pltpu.make_async_copy(own_weights, given.at[0], sems.at[0])]
    loads.append(pltpu.make_async_copy(other_weights, given.at[1], sems.at[0]))
    for c in loads:
        c.start()
    copies = [[], []]
    for half, when, a, b in always:
        copies[half].append((when, pltpu.make_async_copy(a, b, sems.at[1 + half])))
    for when, c in copies[0] + copies[1]:
        pl.when(when)(c.start) if when is not None else c.start()

    for c in loads:
        c.wait()
    places = [(side, g) for side in range(2) for g in range(nz)]
    peaks = [given[side, g, rows : rows + 1, :].astype(F32) for side, g in places]
    peak = functools.reduce(jnp.maximum, peaks)
    for (side, g), own_peak in zip(places, peaks):
        part = (given[side, g, :rows, :].astype(F32) * jnp.exp2(own_peak - peak)).astype(BF)
        weight[county_rows(plan, at, g, side), :] = part
        if side == 0:
            scaled[g] = part

    scaled_copy = pltpu.make_async_copy(scaled, scaled_out, sems.at[0])
    scaled_copy.start()
    blocks, cuts = plan.block_rows, (0, cut // LANES, plan.window // LANES)
    for half in range(2):
        for when, c in copies[half]:
            pl.when(when)(c.wait) if when is not None else c.wait()
        for i in range(blocks):
            for k in range(cuts[half], cuts[half + 1]):
                j = (i + k) % blocks
                tile = strip[i * LANES : (i + 1) * LANES, k * LANES : (k + 1) * LANES]
                full[i * LANES : (i + 1) * LANES, j * LANES : (j + 1) * LANES] = tile
                if k:
                    full[j * LANES : (j + 1) * LANES, i * LANES : (i + 1) * LANES] = tile.T
    copies = [scaled_copy]
    for j in range(nz):
        out = near.at[pl.ds(j * rows, rows)]
        copies.append(
            pltpu.make_async_copy(full.at[county_rows(plan, at, j, 0)], out, sems.at[0])
        )
    for c in copies[1:]:
        c.start()
    def product(j, carry):
        sums[j] = dot(full[county_rows(plan, at, j, 0), :], weight[...])
        return carry

    lax.fori_loop(0, nz, product, 0)
    sent[:, :rows, :] = sums[...].astype(BF)
    sent[:, rows:, :] = jnp.broadcast_to(peak[None], (nz, TILE, plan.wide)).astype(BF)
    for c in copies:
        c.wait()


def share_kernel(plan, masses, totals, out):
    for g in range(plan.n_z):
        total = totals[g, : plan.rows, :].astype(F32)
        out[g] = (masses[g].astype(F32) / total).astype(BF)


def mover_kernel(plan, at, own, other, near, scaled, *refs):
    nz, rows = plan.n_z, plan.rows
    outs, (movers, share, held, sems) = refs[:nz], refs[nz:]
    copies = near_copies(plan, near, held, sems)
    for c in copies:
        c.start()
    for side, x in enumerate((own, other)):
        for g in range(nz):
            share[county_rows(plan, at, g, side), :] = x[g]
    for g in range(nz):
        copies[g].wait()
        arrived = dot(held[g * rows : (g + 1) * rows, :], share[...])
        movers[g] = (scaled[g].astype(F32) * arrived).astype(BF)
    for j in range(nz):
        outs[j][...] = movers[(at[0] // 2) ^ j]


def code_blocks(plan, mix_a, mix_b, ins, mixed):
    rows = plan.rows
    for i, part in enumerate(ins):
        x = part[...]
        new = dot_nt(x, mix_a[...]) + dot_nt(x, mix_b[...])
        most = jnp.maximum(jnp.max(new, axis=0, keepdims=True), 1e-30)
        power = jnp.ceil(jnp.log2(most))
        code = jnp.minimum(jnp.round(new * jnp.exp2(15.0 - power)), HALF - 1.0)
        mixed[:rows, :] = code.astype(jnp.int32)
        mixed[rows:, :] = jnp.broadcast_to(power, (TILE, plan.wide)).astype(jnp.int32)
        yield i


def tail_kernel(plan, at, mix_a, mix_b, *refs):
    ins, outs, mixed = refs[: -1 - plan.n_inc], refs[-1 - plan.n_inc : -1], refs[-1]
    for i in code_blocks(plan, mix_a, mix_b, ins, mixed):
        for k in range(plan.n_inc):
            block = mixed[:, lanes_at((at[1] ^ k) * LANES, LANES)].astype(jnp.int16)
            outs[k][:, i * LANES : (i + 1) * LANES] = block


def next_mass_kernel(plan, at, *refs):
    ni, w, rows = plan.n_inc, plan.wide, plan.rows
    ins, (first, second, out, held, high, low, done, sem) = refs[:-8], refs[-8:]
    copies = []
    z, inc = at[0] // 2, at[1]
    for k in range(ni):
        j = 0
        for part in ins[k::ni]:
            for i in range(part.shape[1] // LANES):
                held[:, lanes_at((z ^ j) * LANES, LANES)] = part[
                    :, i * LANES : (i + 1) * LANES
                ].astype(jnp.int32)
                j += 1
        code = held[...]
        for part, into in ((code >> 8, high), (code & 255, low)):
            back = dot_nt(part.astype(F32).astype(BF), second[...]).astype(BF)
            for t in range(ni):
                into[t, :, lanes_at((inc ^ k) * LANES, LANES)] = back[:, t * LANES : (t + 1) * LANES]
    for t in range(ni):
        code = dot_nt(high[t], first[...]) * 256.0 + dot_nt(low[t], first[...])
        done[t] = code[:rows, :] * jnp.exp2(code[rows : rows + 1, :] - 15.0)
        copies.append(pltpu.make_async_copy(done.at[t], out.at[:, pl.ds(t * w, w)], sem))
        copies[t].start()
    for c in copies:
        c.wait()


def value_kernel(plan, at, *refs):
    ni, w, rows = plan.n_inc, plan.wide, plan.rows
    ins, (hit, second, flow), (out, held) = refs[:ni], refs[ni : ni + 3], refs[ni + 3 :]
    inc = at[1]
    for k in range(ni):
        back = dot_nt(ins[k][...], second[...]).astype(BF)
        for t in range(ni):
            held[t, :, lanes_at((inc ^ k) * LANES, LANES)] = back[:, t * LANES : (t + 1) * LANES]
    for t in range(ni):
        got = dot_nt(held[t], hit[t])
        peak = got[rows : rows + 1, :] * LN2 + SCORE_SHIFT
        out[:, t * w : (t + 1) * w] = flow[:, t * w : (t + 1) * w] + (peak + jnp.log(got[:rows, :]))


def mix_kernel(plan, trans, out_a, out_b):
    e, oi, ga, w = plan.incomes, plan.own_incomes, plan.group_assets, plan.wide
    grid = lambda shape, axis: lax.broadcasted_iota(jnp.int32, shape, axis)
    raised = trans[...] + jnp.where(grid((e, e), 0) == grid((e, e), 1), 16.0, 0.0)
    prob = (raised / jnp.sum(raised, axis=1, keepdims=True)).T
    lane = grid((e, w), 1)
    place = (grid((e, w), 0) == lane // LANES * oi + lane % oi).astype(BF)
    same = grid((w, w), 0) // oi % ga == grid((w, w), 1) // oi % ga
    top = prob.astype(BF)
    for part, out in ((top, out_a), ((prob - top.astype(F32)).astype(BF), out_b)):
        wide = dot(part, place)
        blocks = [wide[i * oi : (i + 1) * oi] for i in range(plan.n_inc) for _ in range(ga)]
        out[...] = jnp.where(same, jnp.concatenate(blocks, axis=0), 0.0).astype(BF)


def policy_maps(plan, asset_policy, inc):
    ni, oa, a, w = plan.n_inc, plan.own_assets, plan.assets, plan.wide
    own = lax.dynamic_slice_in_dim(asset_policy, inc * plan.own_incomes, plan.own_incomes, 0)
    group = w // a
    row_income = jnp.arange(group, dtype=jnp.int32)[None, :, None]
    own = own.reshape(ni, group, a)
    lane = own // oa * LANES + row_income * oa + own % oa
    lane = lane.reshape(ni, w, 1)
    return (lane == lax.broadcasted_iota(jnp.int32, (ni, w, w), 2)).astype(BF)


def swap(x, axis, n, k):
    return lax.ppermute(x, axis, [(s, s ^ k) for s in range(n)]) if k else x


def exchange(blocks, axis, n, unit=1):
    got = {k: swap(blocks[k], axis, n, k * unit) for k in reversed(range(len(blocks)))}
    return [got[k] for k in range(len(blocks))]


def after(x, y):
    return lax.optimization_barrier((x, y))


def state_split(plan, cont_value, flow_util, move_cost, live_mask, trans_weight, asset_policy, mass):
    ni, nl, nz, rows, n = plan.n_inc, plan.n_loc, plan.n_z, plan.rows, plan.counties
    w, packed, half = plan.wide, plan.packed, plan.half
    S = jax.ShapeDtypeStruct
    loc, inc = lax.axis_index("loc"), lax.axis_index("inc")
    at = jnp.stack([loc, inc]).astype(jnp.int32)
    bind = lambda f: functools.partial(f, plan)
    pass_flops = 2 * rows * plan.columns * w
    solve_flops = 2 * half * n * w
    swap_core = lambda x: swap(x, "loc", nl, 1)
    lines = [list(range(core, nl, 2)) for core in range(2)]
    along_z = lambda x: lax.all_to_all(x, "loc", 0, 0, axis_index_groups=lines)
    ring = n + plan.window - LANES

    (quarter,) = call(
        bind(quarter_kernel),
        [S((plan.quarter, plan.window), BF)],
        [at, move_cost],
        [
            pltpu.VMEM((plan.quarter, n), F32),
            pltpu.VMEM((plan.quarter, ring), BF),
            pltpu.SemaphoreType.DMA,
        ],
        specs=[SMEM, ANY],
    )
    pieces = [swap(quarter, "loc", nl, 2 * j) for j in range(2, nz)]

    first, second = order_maps(plan)
    codes = call(
        bind(encode_kernel),
        [S((rows, w), jnp.int16)] * ni,
        [at, cont_value, first, second],
        [pltpu.VMEM((ni, rows, w), BF)] * 2,
        4 * pass_flops,
    )
    codes = exchange(codes, "inc", ni)
    quarter, _ = after(quarter, codes[1])
    pieces.insert(0, swap(quarter, "loc", nl, 2))

    hit = policy_maps(plan, asset_policy, inc)
    masses = call(
        bind(mass_kernel),
        [S((rows, w), BF)] * ni,
        [at, mass, hit, second],
        [pltpu.VMEM((ni, rows, w), BF)],
        3 * pass_flops,
    )
    mix_a, mix_b = call(
        bind(mix_kernel), [S((w, w), BF)] * 2, [trans_weight], specs=[VMEM]
    )
    masses, codes = after(masses, codes)
    masses = exchange(masses, "inc", ni)

    live = (live_mask > 0).astype(F32)[:, None]
    weights = call(
        bind(weight_kernel),
        [S((nz, packed, w), BF)],
        [at, *codes, mix_a, mix_b, live],
        [pltpu.VMEM((rows, w), jnp.int32)],
        3 * pass_flops,
    )
    weights, _ = after(weights[0], pieces)
    weights = along_z(weights)
    others = swap_core(weights)

    strip, _ = after(jnp.concatenate(pieces), masses)
    left, right = strip[:, : plan.cut], strip[:, plan.cut :]
    left = jnp.concatenate([left, swap(left, "inc", ni, 1)])
    right = jnp.concatenate([right, swap(right, "inc", ni, 2)])
    later_cost, _ = after(move_cost, (left, right))
    (own_near,) = call(
        bind(window_kernel),
        [S((rows, plan.window), BF)],
        [at, later_cost],
        [pltpu.VMEM((rows, ring), BF)],
    )
    near = [own_near, left, swap(left, "inc", ni, 2), right, swap(right, "inc", ni, 1)]
    near = near + [swap_core(x) for x in near]

    masses = call(bind(spread_kernel), [S((nz, rows, w), BF)], [at, *masses])
    masses, weights = after(masses[0], weights)
    masses = along_z(masses)

    totals, scaled, near = call(
        bind(total_kernel),
        [S((nz, packed, w), BF), S((nz, rows, w), BF), S((half, n), BF)],
        [at, weights, others, *near],
        [
            pltpu.VMEM((2, nz, packed, w), BF),
            pltpu.VMEM((nz, rows, w), BF),
            pltpu.VMEM((n, w), BF),
            pltpu.VMEM((n, plan.window), BF),
            pltpu.VMEM((n, n), BF),
            pltpu.VMEM((nz, rows, w), F32),
            pltpu.SemaphoreType.DMA((3,)),
        ],
        solve_flops,
        specs=[SMEM, ANY, ANY] + [ANY] * len(near),
        out_specs=[VMEM, ANY, ANY],
        vmem=46,
    )
    sent = along_z(totals)
    (share,) = call(
        bind(share_kernel), [S((nz, rows, w), BF)], [masses, totals], specs=[VMEM] * 2
    )
    movers = call(
        bind(mover_kernel),
        [S((rows, w), BF)] * nz,
        [at, share, swap_core(share), near, scaled],
        [
            pltpu.VMEM((nz, rows, w), BF),
            pltpu.VMEM((n, w), BF),
            pltpu.VMEM((half, n), BF),
            pltpu.SemaphoreType.DMA((nz,)),
        ],
        solve_flops,
        specs=[SMEM, VMEM, VMEM, ANY, VMEM],
        vmem=56,
    )
    close = [movers[0], swap(movers[1], "loc", nl, 2)]
    far = [swap(movers[2], "loc", nl, 4)]
    for j in range(3, nz):
        last, _ = after(movers[j], sent)
        far.append(swap(last, "loc", nl, 2 * j))

    pack = lambda part, outs, kernel: call(
        bind(kernel),
        outs,
        [at, mix_a, mix_b, *part],
        [pltpu.VMEM((packed, w), jnp.int32)],
        pass_flops,
    )
    close = pack(close, [S((packed, 2 * LANES), jnp.int16)] * ni, tail_kernel)
    close = exchange(close, "inc", ni)
    sent = call(bind(collect_kernel), [S((packed, w), BF)] * ni, [at, sent])
    sent = exchange(sent, "inc", ni)
    (new_value,) = call(
        bind(value_kernel),
        [S((rows, plan.columns), F32)],
        [at, *sent, hit, second, flow_util],
        [pltpu.VMEM((ni, packed, w), BF)],
        2 * pass_flops,
    )
    blocks, ready = close, (close, new_value)
    for part in far:
        part, _ = after(part, ready)
        ready = pack([part], [S((packed, LANES), jnp.int16)] * ni, tail_kernel)
        ready = exchange(ready, "inc", ni)
        blocks = blocks + ready

    (new_mass,) = call(
        bind(next_mass_kernel),
        [S((rows, plan.columns), F32)],
        [at, *blocks, first, second],
        [pltpu.VMEM((packed, w), jnp.int32)]
        + [pltpu.VMEM((ni, packed, w), BF)] * 2
        + [pltpu.VMEM((ni, rows, w), F32), pltpu.SemaphoreType.DMA],
        4 * pass_flops,
        out_specs=[ANY],
    )
    return new_value, new_mass


def gathered(cont_value, flow_util, move_cost, live_mask, trans_weight, asset_policy, mass):
    high = lax.Precision.HIGHEST
    e, a = asset_policy.shape
    raised = trans_weight + 16.0 * jnp.eye(e, dtype=F32)
    trans_prob = raised / jnp.sum(raised, axis=1, keepdims=True)
    onehot = (asset_policy[:, :, None] == jnp.arange(a, dtype=jnp.int32)[None, None, :]).astype(F32)
    moved_rows = lax.all_to_all(cont_value, "inc", split_axis=0, concat_axis=1, tiled=True)
    expect = jnp.einsum("ef,jfb->jeb", trans_prob, moved_rows.reshape(-1, e, a), precision=high)
    chosen_all = jnp.einsum("jeb,eab->jea", expect, onehot, precision=high).reshape(-1, e * a)
    chosen = lax.all_to_all(chosen_all, "inc", split_axis=1, concat_axis=0, tiled=True)
    scores = DISCOUNT * chosen
    live_rows = live_mask[:, None] > 0
    local_max = jnp.max(jnp.where(live_rows, scores, F32(-1e30)), axis=0)
    column_max = lax.pmax(local_max, "loc")
    dest_weight = jnp.where(live_rows, jnp.exp(scores - column_max[None, :]), F32(0.0)).astype(BF)
    kernel = jnp.exp(-move_cost).astype(BF)
    totals = dot(kernel, lax.all_gather(dest_weight, "loc", axis=0, tiled=True))
    new_value = flow_util + column_max[None, :] + jnp.log(totals)
    shares = (mass / totals).astype(BF)
    arrived = lax.psum_scatter(
        lax.dot_general(
            kernel, shares, (((0,), (0,)), ((), ())), preferred_element_type=F32
        ).astype(BF),
        "loc",
        scatter_dimension=0,
        tiled=True,
    ).astype(F32)
    movers = dest_weight.astype(F32) * arrived
    moved_mass = lax.all_to_all(movers, "inc", split_axis=0, concat_axis=1, tiled=True)
    shuffled = jnp.einsum("jea,eab->jeb", moved_mass.reshape(-1, e, a), onehot, precision=high)
    mixed_mass = jnp.einsum("ef,jeb->jfb", trans_prob, shuffled, precision=high).reshape(-1, e * a)
    new_mass = lax.all_to_all(mixed_mass, "inc", split_axis=1, concat_axis=0, tiled=True)
    return new_value, new_mass


def solution(mesh):
    n_loc, n_inc = mesh.shape["loc"], mesh.shape["inc"]

    def shards(*args):
        rows, columns = args[0].shape
        plan = Plan(n_loc, n_inc, args[2].shape[1], rows, columns, *args[5].shape)
        if plan.fits():
            return state_split(plan, *args)
        return gathered(*args)

    split = P("loc", "inc")
    return jax.shard_map(
        shards,
        mesh=mesh,
        in_specs=(split, split, P("loc", None), P("loc"), P(), P(), split),
        out_specs=(split, split),
        check_vma=False,
    )
```
